128 devices in a mesh: rec: 8 (over y, core), tm: 16 (over x, z).
Axes of the slice: x: 4, y: 4, z: 4, core: 2. Of those that a mesh axis runs over, the one named last changes fastest.
Arguments:
- loader_rows: bfloat16 [8, 32768, 1024], P('rec', 'tm'), may hold values from -6 to 6
- frame_counts: int32 [8, 16, 16], P('rec'), may hold values from 0 to 128, as said below
- lengths: int32 [8], P('rec'), may hold values from 8193 to 16384, as said below
- cotangent: bfloat16 [8, 16384, 1024], P('rec', 'tm'), may hold values from -6 to 6
- norm_gain: float32 [1024], replicated, may hold values from 0.5 to 1.5
- w_expand: bfloat16 [1024, 2048], replicated, may hold values from -0.1875 to 0.1875
- conv_taps: float32 [9, 1024], replicated, may hold values from -2 to 2
- conv_gain: float32 [1024], replicated, may hold values from 0.5 to 1.5
- w_project: bfloat16 [1024, 1024], replicated, may hold values from -0.1875 to 0.1875
Outputs:
- layer_out: bfloat16 [8, 16384, 1024], P('rec', 'tm')
- grad_in: bfloat16 [8, 16384, 1024], P('rec', 'tm')
- grad_expand: float32 [1024, 2048], P('tm')
- grad_project: float32 [1024, 1024], P('tm')
- grad_taps: float32 [9, 1024], replicated
- grad_norm_gain: float32 [1024], replicated
- grad_conv_gain: float32 [1024], replicated
The draws below stay inside these ranges and needn't reach their ends.
Inputs may be any that keep to these rules, and one draw needn't show every extreme that they name: frame_counts[r, j, k] rows of bucket (j, k) are live, in its first slots; the other slots hold values that are not part of the recording. For every r and k the counts sum over j to exactly 1024, and in every such column some source fills its bucket with 128 rows. `lengths`: in every draw some recording has all 16384 frames.
All inputs are finite; a program needn't handle non-finite values.
Results may differ from the reference program's by a relative error of at most 0.0062.
Values may be sent and summed in bfloat16 or wider, within the bound.
A program may use at most 128 MiB of HBM per device.

```python
import jax
import jax.numpy as jnp
from jax import lax

D = 1024
KER = 9
FR_DEV = 1024
SHARDS = 16
RECS = 8
CAP = 128
NT = 16384


def draw_frame_counts(key, part):
    middle = FR_DEV // SHARDS
    spread = jax.random.randint(jax.random.fold_in(key, 11), (RECS, SHARDS, SHARDS // 2), 0, middle + 1)
    spread = spread.at[:, :, 0].set(middle)
    paired = jnp.stack([middle + spread, middle - spread], axis=-1).reshape(RECS, SHARDS, SHARDS)
    scores = jax.random.randint(jax.random.fold_in(key, 12), (RECS, SHARDS, SHARDS), 0, 1 << 20) * SHARDS
    scores = scores + jnp.arange(SHARDS, dtype=jnp.int32)
    ranking = jnp.argsort(scores, axis=-1, stable=True)
    shuffled = jnp.take_along_axis(paired, ranking, axis=-1)
    return jnp.transpose(shuffled, (0, 2, 1)).astype(jnp.int32)


def draw_lengths(key, part):
    frames_all = FR_DEV * SHARDS
    shortfall = jax.random.randint(jax.random.fold_in(key, 21), (RECS,), 0, frames_all // 2)
    longest = jax.random.randint(jax.random.fold_in(key, 22), (), 0, RECS)
    return jnp.where(jnp.arange(RECS) == longest, frames_all, frames_all - shortfall).astype(jnp.int32)


def strengthened(entries, own_key, source, target, blocks, factor):
    owner, partner = [(jnp.arange(entries.shape[axis_at]) // (entries.shape[axis_at] // blocks)).reshape([-1 if axis == axis_at else 1 for axis in range(entries.ndim)]) for axis_at in (source, target)]
    chosen = jax.random.permutation(own_key, blocks)[partner]
    strong = (owner == chosen) | (owner == (partner + blocks // 2) % blocks)
    return jnp.where(strong, factor * entries, entries)


def block_scale(stream_key, extent, split, least, largest):
    loudness = 1.0
    for dim, shards_of in split:
        heights = jax.random.uniform(jax.random.fold_in(jax.random.fold_in(stream_key, 6), dim), (shards_of,), jnp.float32, least / len(split), largest / len(split))
        loudness = loudness * jnp.repeat(jnp.exp(heights), extent[dim] // shards_of).reshape((-1,) + (1,) * (len(extent) - 1 - dim))
    return loudness


def normal_values(rng, shape, scale, reach, split=(), kind=jnp.bfloat16):
    values = scale * jax.random.normal(rng, shape, jnp.float32)
    if split:
        values = values * block_scale(rng, shape, split, -0.22, 0.18)
    return jnp.clip(values, -reach, reach).astype(kind)


def bell_draw_with(key, extent, scale, most, split, heavy, kind=jnp.bfloat16):
    drawn = scale * jax.random.normal(key, extent, jnp.float32)
    if split:
        drawn = drawn * block_scale(key, extent, split, -0.22, 0.18)
    return jnp.clip(strengthened(drawn, jax.random.fold_in(key, 3), *heavy), -most, most).astype(kind)


def setup_inputs(seed: int = 0) -> dict:
    splits = jax.random.split(jax.random.key(seed), 10)
    loader_rows = bell_draw_with(splits[0], (RECS, SHARDS * SHARDS * CAP, D), 1.0, 6.0, ((0, 8), (1, 16)), (1, 2, 16, 2.0))
    frame_counts = draw_frame_counts(jax.random.fold_in(splits[9], 71), 0)
    lengths = draw_lengths(jax.random.fold_in(splits[9], 71), 0)
    cotangent = normal_values(splits[3], (RECS, NT, D), 1.0, 6.0, ((0, 8), (1, 16)))
    norm_gain = jnp.clip(1.0 + 0.1 * jax.random.normal(splits[4], (D,), jnp.float32), 0.5, 1.5)
    w_expand = normal_values(splits[5], (D, 2 * D), D ** -0.5, 0.1875)
    conv_taps = normal_values(splits[6], (KER, D), KER ** -0.5, 2.0, (), jnp.float32)
    conv_gain = jnp.clip(1.0 + 0.1 * jax.random.normal(splits[7], (D,), jnp.float32), 0.5, 1.5)
    w_project = normal_values(splits[8], (D, D), D ** -0.5, 0.1875)
    return dict(loader_rows=loader_rows, frame_counts=frame_counts, lengths=lengths, cotangent=cotangent, norm_gain=norm_gain, w_expand=w_expand, conv_taps=conv_taps, conv_gain=conv_gain, w_project=w_project)


EPS = 1e-05

def normalize(values):
    center = values - lax.optimization_barrier(jnp.mean(values, axis=-1, keepdims=True))
    inverse = lax.rsqrt(lax.optimization_barrier(jnp.mean(center * center, axis=-1, keepdims=True)) + EPS)
    return (center * inverse, inverse)

def norm_back(grad_norm, normed, inverse):
    return inverse * (grad_norm - lax.optimization_barrier(jnp.mean(grad_norm, axis=-1, keepdims=True)) - normed * lax.optimization_barrier(jnp.mean(grad_norm * normed, axis=-1, keepdims=True)))

def contract_rows(left, right):
    return lax.dot_general(left, right, (((0,), (0,)), ((), ())), preferred_element_type=jnp.float32)

def contract_cols(left, right):
    return lax.dot_general(left, right, (((1,), (1,)), ((), ())), preferred_element_type=jnp.float32)

def regroup_record(loader_rec, counts_rec):
    run_ends = jnp.cumsum(counts_rec, axis=0).astype(jnp.int32)
    starts = (run_ends - counts_rec).astype(jnp.int32)
    position = jnp.arange(FR_DEV, dtype=jnp.int32)
    source = lax.optimization_barrier(jnp.sum((run_ends[:, :, None] <= position[None, None, :]).astype(jnp.int32), axis=0))
    first_slot = jnp.take_along_axis(starts, source.T, axis=0).T
    shard_ids = jnp.arange(SHARDS, dtype=jnp.int32)[:, None]
    row_index = source * (SHARDS * CAP) + shard_ids * CAP + position[None, :] - first_slot
    return loader_rec[row_index.reshape(-1).astype(jnp.int32)]

def layer(sequence, valid_mask, cotangent, norm_gain, w_expand, conv_taps, conv_gain, w_project):
    frames = sequence.shape[0]
    channels = sequence.shape[1]
    taps_count = conv_taps.shape[0]
    margin = taps_count // 2
    inputs = sequence.astype(jnp.float32)
    normed_in, inverse_in = normalize(inputs)
    scaled_in = (normed_in * norm_gain).astype(jnp.bfloat16)
    expanded = jnp.dot(scaled_in, w_expand, preferred_element_type=jnp.float32)
    linear = expanded[:, :channels]
    gate_sig = jax.nn.sigmoid(expanded[:, channels:])
    glu_out = (linear * gate_sig * valid_mask).astype(jnp.bfloat16)
    glu_rim = jnp.pad(glu_out, ((margin, margin), (0, 0)))
    depthwise = jnp.zeros((frames, channels), jnp.float32)
    for kernel_tap in range(taps_count):
        depthwise = depthwise + conv_taps[kernel_tap] * glu_rim[kernel_tap:kernel_tap + frames].astype(jnp.float32)
    normed_conv, inverse_conv = normalize(depthwise)
    scaled_conv = normed_conv * conv_gain
    swish_sig = jax.nn.sigmoid(scaled_conv)
    swished = (scaled_conv * swish_sig).astype(jnp.bfloat16)
    projected = jnp.dot(swished, w_project, preferred_element_type=jnp.float32)
    layer_out = ((inputs + projected) * valid_mask).astype(jnp.bfloat16)
    grad_out = jnp.where(valid_mask > 0.5, cotangent, jnp.zeros_like(cotangent))
    grad_project = contract_rows(swished, grad_out)
    grad_swished = contract_cols(grad_out, w_project)
    grad_scaled_conv = grad_swished * swish_sig * (1.0 + scaled_conv * (1.0 - swish_sig))
    grad_conv_gain = lax.optimization_barrier(jnp.sum(grad_scaled_conv * normed_conv, axis=0))
    grad_depth = norm_back(grad_scaled_conv * conv_gain, normed_conv, inverse_conv)
    depth_rim = jnp.pad(grad_depth, ((margin, margin), (0, 0)))
    grad_taps = jnp.stack([lax.optimization_barrier(jnp.sum(grad_depth * glu_rim[kernel_tap:kernel_tap + frames].astype(jnp.float32), axis=0)) for kernel_tap in range(taps_count)])
    grad_glu = jnp.zeros((frames, channels), jnp.float32)
    for kernel_tap in range(taps_count):
        offset = 2 * margin - kernel_tap
        grad_glu = grad_glu + conv_taps[kernel_tap] * depth_rim[offset:offset + frames]
    grad_glu = grad_glu * valid_mask
    grad_expanded = jnp.concatenate([grad_glu * gate_sig, grad_glu * linear * gate_sig * (1.0 - gate_sig)], axis=1).astype(jnp.bfloat16)
    grad_expand = contract_rows(scaled_in, grad_expanded)
    grad_scaled_in = contract_cols(grad_expanded, w_expand)
    grad_norm_gain = lax.optimization_barrier(jnp.sum(grad_scaled_in * normed_in, axis=0))
    grad_in = (grad_out.astype(jnp.float32) + norm_back(grad_scaled_in * norm_gain, normed_in, inverse_in)).astype(jnp.bfloat16)
    return (layer_out, grad_in, grad_expand, grad_project, grad_taps, grad_norm_gain, grad_conv_gain)

def reference(loader_rows, frame_counts, lengths, cotangent, norm_gain, w_expand, conv_taps, conv_gain, w_project):
    frames_all = FR_DEV * SHARDS

    def one_record(carry, inputs):
        loader_rec, counts_rec, length, cot_rec = inputs
        sequence = regroup_record(loader_rec, counts_rec)
        valid_mask = (jnp.arange(frames_all, dtype=jnp.int32) < length).astype(jnp.float32)[:, None]
        result = layer(sequence, valid_mask, cot_rec, norm_gain, w_expand, conv_taps, conv_gain, w_project)
        carry = jax.tree.map(jnp.add, carry, tuple(result[2:]))
        return (carry, (result[0], result[1]))
    start = (jnp.zeros((D, 2 * D), jnp.float32), jnp.zeros((D, D), jnp.float32), jnp.zeros((KER, D), jnp.float32), jnp.zeros((D,), jnp.float32), jnp.zeros((D,), jnp.float32))
    sums, stacked = lax.scan(one_record, start, (loader_rows, frame_counts, lengths, cotangent))
    return (stacked[0], stacked[1], sums[0], sums[1], sums[2], sums[3], sums[4])
```

```python
import functools

import jax
import jax.numpy as jnp
from jax import lax
from jax.experimental import pallas as pl
from jax.experimental.pallas import tpu as pltpu
from jax.sharding import PartitionSpec as P

EPS = 1e-05
MESH = pl.DeviceIdType.MESH
DMA = pltpu.SemaphoreType.DMA
F32 = jnp.float32
BF16 = jnp.bfloat16
D = 1024
FR = 1024
CAP = 128
KER = 9
HALO = 8
EXT = FR + 2 * HALO
VMEM_LIMIT = 60 * 1024 * 1024


def place():
    rec, tm = lax.axis_index("rec"), lax.axis_index("tm")
    return rec // 2, rec % 2, tm // 4, tm % 4


def device(y, core, x, z):
    return (lax.rem(y + 4, 4) * 2 + core, lax.rem(x + 4, 4) * 4 + lax.rem(z + 4, 4))


def greet(devices):
    barrier = pltpu.get_barrier_semaphore()
    for d in devices:
        pl.semaphore_signal(barrier, inc=1, device_id=d, device_id_type=MESH)
    pl.semaphore_wait(barrier, len(devices))


def contract_rows(left, right):
    return lax.dot_general(left, right, (((0,), (0,)), ((), ())), preferred_element_type=F32)


def contract_cols(left, right):
    return lax.dot_general(left, right, (((1,), (1,)), ((), ())), preferred_element_type=F32)


def row_frames(start, rows):
    row = start + lax.broadcasted_iota(jnp.int32, (rows, 1), 0)
    return jnp.where(row < FR + HALO, row, row - EXT)


OFFSETS = [(dx, dz) for dx in range(4) for dz in range(4) if (dx, dz) != (0, 0)]
SIGNED = (0, 1, None, -1)


def routes():
    out = []
    for dx, dz in OFFSETS:
        for half in (0, 1):
            sign = 1 - 2 * half
            step_x, step_z = (sign if d == 2 else SIGNED[d] for d in (dx, dz))
            along_x = [(step_x, 0)] * (0 if dx == 0 else 2 if dx == 2 else 1)
            along_z = [(0, step_z)] * (0 if dz == 0 else 2 if dz == 2 else 1)
            hops = along_x + along_z if half == 0 else along_z + along_x
            out.append(((dx, dz), half, hops))
    return sorted(out, key=lambda r: -len(r[2]))


ROUTES = routes()
N_HOPS = sum(len(r[2]) for r in ROUTES)
N_RELAY = sum(len(r[2]) - 1 for r in ROUTES)
PIECE = CAP // 2


def regroup_kernel(
    loader, cot, counts, length, w_project, seq, gsw,
    arrived, relay, cot_v, edge, wp_v, send, recv, local, edge_sem,
):
    y, core, x, z = place()
    me = x * 4 + z
    greet([device(y, core, x + dx, z + dz) for dx, dz in OFFSETS])

    hop_id, slot = {}, {}
    for i, (_, _, hops) in enumerate(ROUTES):
        for k in range(len(hops)):
            hop_id[i, k] = len(hop_id)
            if k < len(hops) - 1:
                slot[i, k] = len(slot)
    copies = {}

    def launch(i, k, src):
        (dx, dz), half, hops = ROUTES[i]
        gone_x, gone_z = (sum(h[a] for h in hops[:k]) for a in (0, 1))
        if k == len(hops) - 1:
            origin = lax.rem(x - gone_x + 4, 4) * 4 + lax.rem(z - gone_z + 4, 4)
            dst = arrived.at[pl.ds(origin * CAP + half * PIECE, PIECE)]
        else:
            dst = relay.at[pl.ds(slot[i, k] * PIECE, PIECE)]
        j = hop_id[i, k]
        copies[i, k] = pltpu.make_async_remote_copy(
            src, dst, send.at[j], recv.at[j],
            device_id=device(y, core, x + hops[k][0], z + hops[k][1]), device_id_type=MESH,
        )
        copies[i, k].start()

    for i, ((dx, dz), half, _) in enumerate(ROUTES):
        to = lax.rem(x + dx, 4) * 4 + lax.rem(z + dz, 4)
        launch(i, 0, loader.at[pl.ds(to * CAP + half * PIECE, PIECE)])
    own = pltpu.make_async_copy(loader.at[pl.ds(me * CAP, CAP)], arrived.at[pl.ds(me * CAP, CAP)], local.at[0])
    own.start()
    left = device(y, core, lax.rem(me + 15, 16) // 4, lax.rem(me + 15, 16) % 4)
    right = device(y, core, lax.rem(me + 1, 16) // 4, lax.rem(me + 1, 16) % 4)
    get_cot = pltpu.make_async_copy(cot, cot_v, local.at[1])
    get_wp = pltpu.make_async_copy(w_project, wp_v, local.at[2])
    get_cot.start()
    get_wp.start()
    first = pltpu.make_async_remote_copy(
        cot.at[pl.ds(0, 16)], edge.at[0], edge_sem.at[0], edge_sem.at[1], device_id=left, device_id_type=MESH)
    last = pltpu.make_async_remote_copy(
        cot.at[pl.ds(FR - 16, 16)], edge.at[1], edge_sem.at[2], edge_sem.at[3], device_id=right, device_id_type=MESH)
    first.start()
    last.start()
    live = length[0] - me * FR
    get_cot.wait()
    get_wp.wait()

    @pl.loop(0, 4)
    def _(k):
        r0 = pl.multiple_of(k * 256, 256)
        frame = r0 + lax.broadcasted_iota(jnp.int32, (256, 1), 0)
        tile = cot_v[pl.ds(r0, 256)]
        tile = jnp.where(frame < live, tile, jnp.zeros_like(tile))
        gsw[pl.ds(r0, 256)] = contract_cols(tile, wp_v[...])

    first.wait()
    last.wait()
    rim = jnp.concatenate([edge[0].astype(F32)[:HALO], edge[1].astype(F32)[16 - HALO :]], axis=0)
    frame = row_frames(FR, 2 * HALO)
    rim = jnp.where((frame < live) & (frame + me * FR >= 0), rim, 0.0).astype(BF16)
    gsw[pl.ds(FR, 2 * HALO)] = contract_cols(rim, wp_v[...])

    for k in range(1, 4):
        for i, (_, _, hops) in enumerate(ROUTES):
            if k < len(hops):
                copies[i, k - 1].wait_recv()
                launch(i, k, relay.at[pl.ds(slot[i, k - 1] * PIECE, PIECE)])
    own.wait()
    for (i, k), copy in copies.items():
        copy.wait_send()
        if k == len(ROUTES[i][2]) - 1:
            copy.wait_recv()

    begin = jnp.int32(0)
    places = []
    lane = lax.broadcasted_iota(jnp.int32, (1, CAP), 1)
    for j in range(16):
        count = counts[j, me]
        places.append(jnp.where(lane < count, begin + lane, -1))
        begin = begin + count
    places = jnp.concatenate(places, axis=1)

    @pl.loop(0, 4)
    def _(k):
        r0 = pl.multiple_of(k * 256, 256)
        frame = r0 + lax.broadcasted_iota(jnp.int32, (256, 1), 0)
        pick = jnp.where(frame == places, 1.0, 0.0).astype(BF16)
        seq[pl.ds(r0, 256)] = jnp.dot(pick, arrived[...], preferred_element_type=F32)

    first = pltpu.make_async_remote_copy(
        seq.at[pl.ds(0, HALO)], seq.at[pl.ds(FR, HALO)], edge_sem.at[4], edge_sem.at[5], device_id=left, device_id_type=MESH)
    last = pltpu.make_async_remote_copy(
        seq.at[pl.ds(FR - HALO, HALO)], seq.at[pl.ds(FR + HALO, HALO)], edge_sem.at[6], edge_sem.at[7], device_id=right, device_id_type=MESH)
    first.start()
    last.start()
    first.wait()
    last.wait()


def regroup(loader, cot, counts, length, w_project):
    any_space = pl.BlockSpec(memory_space=pl.ANY)
    vmem = pl.BlockSpec(memory_space=pltpu.VMEM)
    smem = pl.BlockSpec(memory_space=pltpu.SMEM)
    return pl.pallas_call(
        regroup_kernel,
        out_shape=[jax.ShapeDtypeStruct((EXT, D), F32), jax.ShapeDtypeStruct((EXT, D), F32)],
        in_specs=[any_space, any_space, smem, smem, any_space],
        out_specs=[vmem, vmem],
        scratch_shapes=[
            pltpu.VMEM((16 * CAP, D), BF16),
            pltpu.VMEM((N_RELAY * PIECE, D), BF16),
            pltpu.VMEM((FR, D), BF16),
            pltpu.VMEM((2, 16, D), BF16),
            pltpu.VMEM((D, D), BF16),
            DMA((N_HOPS,)),
            DMA((N_HOPS,)),
            DMA((3,)),
            DMA((8,)),
        ],
        compiler_params=pltpu.CompilerParams(collective_id=0, has_side_effects=True, vmem_limit_bytes=VMEM_LIMIT),
    )(loader, cot, counts, length, w_project)


def mean(values):
    return jnp.mean(values, axis=-1, keepdims=True)


def normalize(values):
    center = values - mean(values)
    inverse = lax.rsqrt(mean(center * center) + EPS)
    return center * inverse, inverse


def norm_back(grad, normed, inverse):
    return inverse * (grad - mean(grad) - normed * mean(grad * normed))


def fold(values):
    return jnp.sum(values.reshape(-1, 8, values.shape[-1]), axis=0)


T1 = 208
RT = 64
CC = 256


def shard_kernel(
    length, seq, gsw, cot, norm_gain, w_expand, taps, conv_gain, w_project,
    layer_out, grad_in, weights, small,
    glu, lin, gate, scaled, dgrad, swished, gout, gexp, dw, tapsum, gainsum,
):
    me = lax.axis_index("tm")
    live = length[0] - me * FR

    @pl.loop(0, EXT // T1)
    def _(k):
        r0 = pl.multiple_of(k * T1, 16)
        normed, _ = normalize(seq[pl.ds(r0, T1)])
        s = (normed * norm_gain[...]).astype(BF16)
        scaled[pl.ds(r0, T1)] = s
        frame = row_frames(r0, T1)
        valid = (frame < live) & (frame + me * FR >= 0)
        for c in range(0, D, 512):
            a = jnp.dot(s, w_expand[:, c : c + 512], preferred_element_type=F32)
            b = jax.nn.sigmoid(jnp.dot(s, w_expand[:, D + c : D + c + 512], preferred_element_type=F32))
            lin[pl.ds(r0, T1), c : c + 512] = a
            gate[pl.ds(r0, T1), c : c + 512] = b
            glu[pl.ds(r0 + 16, T1), c : c + 512] = jnp.where(valid, a * b, 0.0).astype(BF16).astype(F32)

    glu[pl.ds(8, 8)] = glu[pl.ds(16 + FR + HALO, 8)]
    glu[pl.ds(0, 8)] = jnp.zeros((8, D), F32)
    gainsum[...] = jnp.zeros_like(gainsum)
    tapsum[...] = jnp.zeros_like(tapsum)

    def middle(at, rows, gs_at):
        for c in range(0, D, CC):
            wide = glu[pl.ds(at - 8, rows + 16), c : c + CC]
            acc = taps[0:1, c : c + CC] * wide[4 : 4 + rows]
            for t in range(1, KER):
                acc = acc + taps[t : t + 1, c : c + CC] * wide[4 + t : 4 + t + rows]
            dw[pl.ds(0, rows), c : c + CC] = acc
        normed, inverse = normalize(dw[pl.ds(0, rows)])
        sc = normed * conv_gain[...]
        sig = jax.nn.sigmoid(sc)
        gsc = gsw[pl.ds(gs_at, rows)] * sig * (1.0 + sc * (1.0 - sig))
        dgrad[pl.ds(at, rows)] = norm_back(gsc * conv_gain[...], normed, inverse)
        return sc * sig, gsc * normed

    @pl.loop(0, FR // RT)
    def _(k):
        r0 = pl.multiple_of(k * RT, RT)
        sw, gc = middle(pl.multiple_of(r0 + 16, 16), RT, r0)
        swished[pl.ds(r0, RT)] = sw.astype(BF16)
        gainsum[0] += fold(gc)

    middle(16 + FR, HALO, FR)
    middle(8 + 0, HALO, FR + HALO)

    @pl.loop(0, 4)
    def _(k):
        r0 = pl.multiple_of(k * 256, 256)
        frame = r0 + lax.broadcasted_iota(jnp.int32, (256, 1), 0)
        tile = cot[pl.ds(r0, 256)]
        gout[pl.ds(r0, 256)] = jnp.where(frame < live, tile, jnp.zeros_like(tile))
        projected = jnp.dot(swished[pl.ds(r0, 256)], w_project[...], preferred_element_type=F32)
        layer_out[pl.ds(r0, 256)] = jnp.where(frame < live, seq[pl.ds(r0, 256)] + projected, 0.0).astype(BF16)

    @pl.loop(0, 4)
    def _(k):
        c0 = pl.multiple_of(k * 256, 256)
        weights[pl.ds(c0, 256), 2 * D :] = contract_rows(swished[:, pl.ds(c0, 256)], gout[...]).astype(BF16)

    @pl.loop(0, FR // RT)
    def _(k):
        r0 = pl.multiple_of(k * RT, RT)
        frame = r0 + lax.broadcasted_iota(jnp.int32, (RT, 1), 0)
        for c in range(0, D, CC):
            wide = dgrad[pl.ds(pl.multiple_of(r0 + 8, 8), RT + 16), c : c + CC]
            mid = glu[pl.ds(pl.multiple_of(r0 + 16, 16), RT), c : c + CC]
            acc = jnp.zeros((RT, CC), F32)
            for t in range(KER):
                shifted = wide[12 - t : 12 - t + RT]
                acc = acc + taps[t : t + 1, c : c + CC] * shifted
                tapsum[t, :, c : c + CC] += fold(mid * shifted)
            a = lin[pl.ds(r0, RT), c : c + CC]
            b = gate[pl.ds(r0, RT), c : c + CC]
            gg = jnp.where(frame < live, acc, 0.0) * b
            gexp[pl.ds(r0, RT), c : c + CC] = gg.astype(BF16)
            gexp[pl.ds(r0, RT), D + c : D + c + CC] = (gg * a * (1.0 - b)).astype(BF16)

    @pl.loop(0, 4)
    def _(k):
        c0 = pl.multiple_of(k * 256, 256)
        for c in range(0, 2 * D, 1024):
            weights[pl.ds(c0, 256), c : c + 1024] = contract_rows(
                scaled[pl.ds(0, FR), pl.ds(c0, 256)], gexp[:, c : c + 1024]).astype(BF16)

    @pl.loop(0, 4)
    def _(k):
        r0 = pl.multiple_of(k * 256, 256)
        grad_scaled = contract_cols(gexp[pl.ds(r0, 256)], w_expand[...])
        normed, inverse = normalize(seq[pl.ds(r0, 256)])
        gainsum[1] += fold(grad_scaled * normed)
        grad_in[pl.ds(r0, 256)] = (
            gout[pl.ds(r0, 256)].astype(F32) + norm_back(grad_scaled * norm_gain[...], normed, inverse)
        ).astype(BF16)

    small[...] = jnp.zeros_like(small)
    for t in range(KER):
        small[t : t + 1] = jnp.sum(tapsum[t], axis=0, keepdims=True)
    small[9:10] = jnp.sum(gainsum[1], axis=0, keepdims=True)
    small[10:11] = jnp.sum(gainsum[0], axis=0, keepdims=True)


def shard_work(length, seq, gsw, cot, norm_gain, w_expand, taps, conv_gain, w_project):
    vmem = pl.BlockSpec(memory_space=pltpu.VMEM)
    smem = pl.BlockSpec(memory_space=pltpu.SMEM)
    rows = FR + 2 * 16
    return pl.pallas_call(
        shard_kernel,
        out_shape=[
            jax.ShapeDtypeStruct((FR, D), BF16),
            jax.ShapeDtypeStruct((FR, D), BF16),
            jax.ShapeDtypeStruct((D, 3 * D), BF16),
            jax.ShapeDtypeStruct((16, D), F32),
        ],
        in_specs=[smem] + [vmem] * 8,
        out_specs=[vmem] * 4,
        scratch_shapes=[
            pltpu.VMEM((rows, D), F32),
            pltpu.VMEM((EXT, D), F32),
            pltpu.VMEM((EXT, D), F32),
            pltpu.VMEM((EXT, D), BF16),
            pltpu.VMEM((rows, D), F32),
            pltpu.VMEM((FR, D), BF16),
            pltpu.VMEM((FR, D), BF16),
            pltpu.VMEM((FR, 2 * D), BF16),
            pltpu.VMEM((RT, D), F32),
            pltpu.VMEM((KER, 8, D), F32),
            pltpu.VMEM((2, 8, D), F32),
        ],
        compiler_params=pltpu.CompilerParams(vmem_limit_bytes=VMEM_LIMIT),
    )(length, seq, gsw, cot, norm_gain, w_expand, taps, conv_gain, w_project)


ORDERS = (("x", "z", "y"), ("z", "y", "x"), ("y", "x", "z"))
COLS = 512
HALF = COLS // 2


def sum_kernel(
    weights, small, out_expand, out_project, out_small,
    mine, part, hop1, hop2, final, pair_small, ring_small, full_small,
    load_sem, pair_sem, hop_send, hop_recv, fin_sem, sm_sem,
):
    y, core, x, z = place()
    pos = {"x": x, "y": y, "z": z}

    def along(axis, by):
        at = dict(pos)
        at[axis] = pos[axis] + by
        return device(at["y"], core, at["x"], at["z"])

    partner = device(y, 1 - core, x, z)
    greet([partner] + [along(a, b) for a in "xyz" for b in (1, 2, 3)])

    loads, pairs = [], []
    for p in range(3):
        away = pl.multiple_of((1 - core) * 1536 + p * COLS, COLS)
        c = pltpu.make_async_remote_copy(
            weights.at[:, :, :, :, pl.ds(away, COLS)], part.at[p], pair_sem.at[0, p], pair_sem.at[1, p],
            device_id=partner, device_id_type=MESH)
        c.start()
        pairs.append(c)
        here = pl.multiple_of(core * 1536 + p * COLS, COLS)
        c = pltpu.make_async_copy(weights.at[:, :, :, :, pl.ds(here, COLS)], mine.at[p], load_sem.at[p])
        c.start()
        loads.append(c)
    away = pl.multiple_of((1 - core) * 512, 512)
    here = pl.multiple_of(core * 512, 512)
    small_pair = pltpu.make_async_remote_copy(
        small.at[:, pl.ds(away, 512)], pair_small, sm_sem.at[0, 0], sm_sem.at[1, 0], device_id=partner, device_id_type=MESH)
    small_pair.start()
    done = []

    def view(p, s, c, cols):
        index = {"x": slice(None), "z": slice(None), "y": slice(None)}
        for a in ORDERS[p][:s]:
            index[a] = pos[a]
        index[ORDERS[p][s]] = lax.rem(c + 4, 4)
        return (p, index["x"], index["z"], index["y"], slice(None), cols)

    LO, HI = pl.ds(0, HALF), pl.ds(HALF, HALF)

    def buffer(ref, p, s, k):
        return ref[s].at[p, k]

    def start(p, s, n, src, dst, by):
        c = pltpu.make_async_remote_copy(
            src, dst, hop_send.at[p, s, n], hop_recv.at[p, s, n],
            device_id=along(ORDERS[p][s], by), device_id_type=MESH)
        c.start()
        return c

    def small_stage(s, axis, value):
        buf = ring_small.at[s]
        buf[pos[axis]] = value
        out = []
        for by in (1, 2, 3):
            c = pltpu.make_async_remote_copy(
                buf.at[pos[axis]], buf.at[pos[axis]], sm_sem.at[0, 1 + 3 * s + by - 1], sm_sem.at[1, 1 + 3 * s + by - 1],
                device_id=along(axis, by), device_id_type=MESH)
            c.start()
            out.append(c)
        return out

    def small_sum(s, copies):
        for c in copies:
            c.wait()
        b = ring_small.at[s]
        return (b[0] + b[1]) + (b[2] + b[3])

    small_value = small_copies = None
    stage = {}
    for s in range(3):
        for p in range(3):
            if s == 0:
                loads[p].wait()
                pairs[p].wait_recv()

                @pl.loop(0, 4)
                def _(i):
                    @pl.loop(0, 4)
                    def _(j):
                        part[p, i, j] = (part[p, i, j].astype(F32) + mine[p, i, j].astype(F32)).astype(BF16)

            m = pos[ORDERS[p][s]]
            stage[p] = [
                start(p, s, 0, part.at[view(p, s, m + 2, LO)], buffer(hop1, p, s, 0), 1),
                start(p, s, 1, part.at[view(p, s, m + 2, HI)], buffer(hop1, p, s, 1), -1),
                start(p, s, 2, part.at[view(p, s, m + 1, HI)], buffer(hop2, p, s, 0), 1),
                start(p, s, 3, part.at[view(p, s, m - 1, LO)], buffer(hop2, p, s, 1), -1),
            ]
        if s == 0:
            small_pair.wait()
            small_value = small[:, pl.ds(here, 512)] + pair_small[...]
        small_copies = small_stage(s, "xzy"[s], small_value)
        for p in range(3):
            m = pos[ORDERS[p][s]]
            stage[p][0].wait_recv()
            at = view(p, s, m + 1, LO)
            part[at] = (part[at].astype(F32) + hop1[s][p, 0].astype(F32)).astype(BF16)
            stage[p].append(start(p, s, 4, part.at[at], buffer(hop2, p, s, 2), 1))
            stage[p][1].wait_recv()
            at = view(p, s, m - 1, HI)
            part[at] = (part[at].astype(F32) + hop1[s][p, 1].astype(F32)).astype(BF16)
            stage[p].append(start(p, s, 5, part.at[at], buffer(hop2, p, s, 3), -1))
        small_value = small_sum(s, small_copies)
        for p in range(3):
            m = pos[ORDERS[p][s]]
            for c in stage[p][2:]:
                c.wait_recv()
            low, high = view(p, s, m, LO), view(p, s, m, HI)
            sum_low = part[low].astype(F32) + hop2[s][p, 2].astype(F32) + hop2[s][p, 1].astype(F32)
            sum_high = part[high].astype(F32) + hop2[s][p, 0].astype(F32) + hop2[s][p, 3].astype(F32)
            if s < 2:
                part[low] = sum_low.astype(BF16)
                part[high] = sum_high.astype(BF16)
            else:
                final[core, y, :, p * COLS : p * COLS + HALF] = sum_low.astype(BF16)
                final[core, y, :, p * COLS + HALF : (p + 1) * COLS] = sum_high.astype(BF16)
            done += stage[p]

    gather = []
    for by in (1, 2, 3):
        c = pltpu.make_async_remote_copy(
            final.at[core, y], final.at[core, y], fin_sem.at[0, by - 1], fin_sem.at[1, by - 1],
            device_id=along("y", by), device_id_type=MESH)
        c.start()
        gather.append(c)
    full_small[core] = small_value
    small_last = pltpu.make_async_remote_copy(
        full_small.at[core], full_small.at[core], sm_sem.at[0, 10], sm_sem.at[1, 10], device_id=partner, device_id_type=MESH)
    small_last.start()
    for c in gather:
        c.wait_recv()
    last = pltpu.make_async_remote_copy(
        final.at[core], final.at[core], fin_sem.at[0, 3], fin_sem.at[1, 3], device_id=partner, device_id_type=MESH)
    last.start()
    small_last.wait()
    out_small[:, 0:512] = full_small[0]
    out_small[:, 512:1024] = full_small[1]
    last.wait()
    for k in range(4):
        rows = slice(k * 16, k * 16 + 16)
        out_expand[rows, 0:1536] = final[0, k].astype(F32)
        out_expand[rows, 1536:2048] = final[1, k][:, 0:512].astype(F32)
        out_project[rows, :] = final[1, k][:, 512:1536].astype(F32)
    for c in gather + pairs + done:
        c.wait_send()


def sum_all(weights, small):
    any_space = pl.BlockSpec(memory_space=pl.ANY)
    vmem = pl.BlockSpec(memory_space=pltpu.VMEM)

    def hop_shapes(n):
        return [pltpu.VMEM((3, n) + (4,) * (2 - s) + (16, HALF), BF16) for s in range(3)]

    return pl.pallas_call(
        lambda w, s, oe, op, os, mine, part, a0, a1, a2, b0, b1, b2, *rest: sum_kernel(
            w, s, oe, op, os, mine, part, (a0, a1, a2), (b0, b1, b2), *rest),
        out_shape=[
            jax.ShapeDtypeStruct((D // 16, 2 * D), F32),
            jax.ShapeDtypeStruct((D // 16, D), F32),
            jax.ShapeDtypeStruct((16, D), F32),
        ],
        in_specs=[any_space, vmem],
        out_specs=[vmem] * 3,
        scratch_shapes=[
            pltpu.VMEM((3, 4, 4, 4, 16, COLS), BF16),
            pltpu.VMEM((3, 4, 4, 4, 16, COLS), BF16),
            *hop_shapes(2),
            *hop_shapes(4),
            pltpu.VMEM((2, 4, 16, 3 * COLS), BF16),
            pltpu.VMEM((16, 512), F32),
            pltpu.VMEM((3, 4, 16, 512), F32),
            pltpu.VMEM((2, 16, 512), F32),
            DMA((3,)),
            DMA((2, 3)),
            DMA((3, 3, 6)),
            DMA((3, 3, 6)),
            DMA((2, 4)),
            DMA((2, 11)),
        ],
        compiler_params=pltpu.CompilerParams(collective_id=1, has_side_effects=True, vmem_limit_bytes=VMEM_LIMIT),
    )(weights.reshape(4, 4, 4, 16, 3 * D), small)


def per_device(
    loader_rows, frame_counts, lengths, cotangent, norm_gain, w_expand, conv_taps, conv_gain, w_project,
):
    seq, gsw = regroup(loader_rows[0], cotangent[0], frame_counts[0], lengths, w_project)
    layer_out, grad_in, weights, small = shard_work(
        lengths, seq, gsw, cotangent[0], norm_gain[None], w_expand, conv_taps, conv_gain[None], w_project)
    expand, project, small = sum_all(weights, small)
    return layer_out[None], grad_in[None], expand, project, small[:KER], small[9], small[10]


def solution(mesh):
    return jax.shard_map(
        per_device,
        mesh=mesh,
        in_specs=(
            P("rec", "tm", None), P("rec", None, None), P("rec"), P("rec", "tm", None),
            P(), P(), P(), P(), P(),
        ),
        out_specs=(
            P("rec", "tm", None), P("rec", "tm", None), P("tm", None), P("tm", None), P(), P(), P(),
        ),
        check_vma=False,
    )
```

```python
import functools

import jax
import jax.numpy as jnp
from jax import lax
from jax.experimental import pallas as pl
from jax.experimental.pallas import tpu as pltpu
from jax.sharding import PartitionSpec as P

EPS = 1e-05
MESH = pl.DeviceIdType.MESH
DMA = pltpu.SemaphoreType.DMA
F32 = jnp.float32
BF16 = jnp.bfloat16
D = 1024
FR = 1024
CAP = 128
KER = 9
HALO = 8
EXT = FR + 2 * HALO
VMEM_LIMIT = 61 * 1024 * 1024


def place():
    rec, tm = lax.axis_index("rec"), lax.axis_index("tm")
    return rec // 2, rec % 2, tm // 4, tm % 4


def device(y, core, x, z):
    return (lax.rem(y + 4, 4) * 2 + core, lax.rem(x + 4, 4) * 4 + lax.rem(z + 4, 4))


def greet(devices):
    barrier = pltpu.get_barrier_semaphore()
    for d in devices:
        pl.semaphore_signal(barrier, inc=1, device_id=d, device_id_type=MESH)
    pl.semaphore_wait(barrier, len(devices))


def contract_rows(left, right):
    return lax.dot_general(left, right, (((0,), (0,)), ((), ())), preferred_element_type=F32)


def contract_cols(left, right):
    return lax.dot_general(left, right, (((1,), (1,)), ((), ())), preferred_element_type=F32)


def row_frames(start, rows):
    row = start + lax.broadcasted_iota(jnp.int32, (rows, 1), 0)
    return jnp.where(row < FR + HALO, row, row - EXT)


OFFSETS = [(dx, dz) for dx in range(4) for dz in range(4) if (dx, dz) != (0, 0)]
SIGNED = (0, 1, None, -1)


def routes():
    out = []
    for dx, dz in OFFSETS:
        for half in (0, 1):
            sign_x = (1 - 2 * half) * (-1 if dz == 3 else 1)
            sign_z = (1 - 2 * half) * (-1 if dx == 1 else 1)
            step_x = sign_x if dx == 2 else SIGNED[dx]
            step_z = sign_z if dz == 2 else SIGNED[dz]
            along_x = [(step_x, 0)] * (0 if dx == 0 else 2 if dx == 2 else 1)
            along_z = [(0, step_z)] * (0 if dz == 0 else 2 if dz == 2 else 1)
            hops = along_x + along_z if half == 0 else along_z + along_x
            out.append(((dx, dz), half, hops))
    return sorted(out, key=lambda r: -len(r[2]))


ROUTES = routes()
N_HOPS = sum(len(r[2]) for r in ROUTES)
N_RELAY = sum(len(r[2]) - 1 for r in ROUTES)
PIECE = CAP // 2


def mean(values):
    return jnp.mean(values, axis=-1, keepdims=True)


def normalize(values):
    center = values - mean(values)
    inverse = lax.rsqrt(mean(center * center) + EPS)
    return center * inverse, inverse


def norm_back(grad, normed, inverse):
    return inverse * (grad - mean(grad) - normed * mean(grad * normed))


def fold(values):
    return jnp.sum(values.reshape(-1, 8, values.shape[-1]), axis=0)


T1 = 208
RC = 80
RB = 64
RT = 64
CC = 128


ORDERS = (("y", "x", "z"), ("x", "z", "y"), ("z", "y", "x"))
COLS = 512
HALF = COLS // 2
LO, HI = pl.ds(0, HALF), pl.ds(HALF, HALF)


def kernel(
    loader, cot, counts, length, norm_gain, w_expand, taps, conv_gain, w_project,
    layer_out, grad_in, relay, out_sum, out_small,
    arrived, cotv, edge, wp, we, seq, gsw, glu, dgrad, lin, gate, scaled, swished, gainsum, small,
    away, pair, part, hop1_0, hop1_1, hop1_2, hop2_0, hop2_1, hop2_2, final, pair_small, ring_small, full_small,
    send, recv, local, edge_sem, pair_sem, hop_send, hop_recv, fin_sem, sm_sem,
):
    hop1, hop2 = (hop1_0, hop1_1, hop1_2), (hop2_0, hop2_1, hop2_2)
    y, core, x, z = place()
    pos = {"x": x, "y": y, "z": z}
    me = x * 4 + z
    live = length[0] - me * FR
    partner = device(y, 1 - core, x, z)

    def along(axis, by):
        at = dict(pos)
        at[axis] = pos[axis] + by
        return device(at["y"], core, at["x"], at["z"])

    greet([device(y, core, x + dx, z + dz) for dx, dz in OFFSETS] + [partner] + [along("y", b) for b in (1, 2, 3)])

    hop_id, slot = {}, {}
    for i, (_, _, hops) in enumerate(ROUTES):
        for k in range(len(hops)):
            hop_id[i, k] = len(hop_id)
            if k < len(hops) - 1:
                slot[i, k] = len(slot)
    copies = {}

    def launch(i, k, src):
        _, half, hops = ROUTES[i]
        gone_x, gone_z = (sum(h[a] for h in hops[:k]) for a in (0, 1))
        if k == len(hops) - 1:
            origin = lax.rem(x - gone_x + 4, 4) * 4 + lax.rem(z - gone_z + 4, 4)
            dst = arrived.at[pl.ds(origin * CAP + half * PIECE, PIECE)]
        else:
            dst = relay.at[pl.ds(slot[i, k] * PIECE, PIECE)]
        j = hop_id[i, k]
        copies[i, k] = pltpu.make_async_remote_copy(
            src, dst, send.at[j], recv.at[j],
            device_id=device(y, core, x + hops[k][0], z + hops[k][1]), device_id_type=MESH,
        )
        copies[i, k].start()

    before, after = lax.rem(me + 15, 16), lax.rem(me + 1, 16)
    left = device(y, core, before // 4, lax.rem(before, 4))
    right = device(y, core, after // 4, lax.rem(after, 4))
    first = pltpu.make_async_remote_copy(
        cot.at[pl.ds(0, 16)], edge.at[0], edge_sem.at[0], edge_sem.at[1], device_id=left, device_id_type=MESH)
    last = pltpu.make_async_remote_copy(
        cot.at[pl.ds(FR - 16, 16)], edge.at[1], edge_sem.at[2], edge_sem.at[3], device_id=right, device_id_type=MESH)
    first.start()
    last.start()
    for i, ((dx, dz), half, _) in enumerate(ROUTES):
        to = lax.rem(x + dx, 4) * 4 + lax.rem(z + dz, 4)
        launch(i, 0, loader.at[pl.ds(to * CAP + half * PIECE, PIECE)])
    own = pltpu.make_async_copy(loader.at[pl.ds(me * CAP, CAP)], arrived.at[pl.ds(me * CAP, CAP)], local.at[0])
    get_cot = pltpu.make_async_copy(cot, cotv, local.at[1])
    get_wp = pltpu.make_async_copy(w_project, wp, local.at[2])
    get_we = pltpu.make_async_copy(w_expand, we, local.at[3])
    for c in (get_cot, get_wp, own, get_we):
        c.start()
    get_cot.wait()
    get_wp.wait()

    @pl.loop(0, 4)
    def _(k):
        r0 = pl.multiple_of(k * 256, 256)
        frame = r0 + lax.broadcasted_iota(jnp.int32, (256, 1), 0)
        tile = cotv[pl.ds(r0, 256)]
        tile = jnp.where(frame < live, tile, jnp.zeros_like(tile))
        cotv[pl.ds(r0, 256)] = tile
        gsw[pl.ds(r0, 256)] = contract_cols(tile, wp[...])

    gainsum[...] = jnp.zeros_like(gainsum)
    small[...] = jnp.zeros_like(small)

    for k in range(1, 4):
        for i, (_, _, hops) in enumerate(ROUTES):
            if k < len(hops):
                copies[i, k - 1].wait_recv()
                launch(i, k, relay.at[pl.ds(slot[i, k - 1] * PIECE, PIECE)])

    first.wait()
    last.wait()
    rim = jnp.concatenate([edge[0].astype(F32)[:HALO], edge[1].astype(F32)[16 - HALO :]], axis=0)
    frame = row_frames(FR, 2 * HALO)
    rim = jnp.where((frame < live) & (frame + me * FR >= 0), rim, 0.0).astype(BF16)
    gsw[pl.ds(FR, 2 * HALO)] = contract_cols(rim, wp[...])
    column = [counts[j, me] for j in range(16)]
    lane = lax.broadcasted_iota(jnp.int32, (1, CAP), 1)

    def collect(offsets, fresh):
        origins, places = [], []
        for dx, dz in offsets:
            origin = lax.rem(x - dx + 4, 4) * 4 + lax.rem(z - dz + 4, 4)
            begin = count = jnp.int32(0)
            for j in range(16):
                begin = begin + jnp.where(j < origin, column[j], 0)
                count = count + jnp.where(j == origin, column[j], 0)
            origins.append(origin)
            places.append(jnp.where(lane < count, begin + lane, -1))
        places = jnp.concatenate(places, axis=1)

        @pl.loop(0, 4)
        def _(k):
            r0 = pl.multiple_of(k * 256, 256)
            frame = r0 + lax.broadcasted_iota(jnp.int32, (256, 1), 0)
            pick = jnp.where(frame == places, 1.0, 0.0).astype(BF16)
            rows = jnp.concatenate([arrived[pl.ds(pl.multiple_of(o * CAP, CAP), CAP)] for o in origins], axis=0)
            got = jnp.dot(pick, rows, preferred_element_type=F32)
            seq[pl.ds(r0, 256)] = got if fresh else seq[pl.ds(r0, 256)] + got

    own.wait()
    for n, some in enumerate(((3, 4), (2,), (1,))):
        here = []
        for i, (offset, _, hops) in enumerate(ROUTES):
            if len(hops) in some:
                copies[i, len(hops) - 1].wait_recv()
                if offset not in here:
                    here.append(offset)
        collect(here + [(0, 0)] * (n == 0), n == 0)

    first = pltpu.make_async_remote_copy(
        seq.at[pl.ds(0, HALO)], seq.at[pl.ds(FR, HALO)], edge_sem.at[4], edge_sem.at[5], device_id=left, device_id_type=MESH)
    last = pltpu.make_async_remote_copy(
        seq.at[pl.ds(FR - HALO, HALO)], seq.at[pl.ds(FR + HALO, HALO)], edge_sem.at[6], edge_sem.at[7], device_id=right, device_id_type=MESH)
    first.start()
    last.start()
    get_we.wait()

    @pl.loop(0, EXT // T1)
    def _(k):
        @pl.when(k == EXT // T1 - 1)
        def _():
            first.wait()
            last.wait()

        r0 = pl.multiple_of(k * T1, 16)
        normed, _ = normalize(seq[pl.ds(r0, T1)])
        scaled[pl.ds(r0, T1)] = (normed * norm_gain[...]).astype(BF16)
        frame = row_frames(r0, T1)
        valid = (frame < live) & (frame + me * FR >= 0)

        @pl.loop(0, 2)
        def _(h):
            c = pl.multiple_of(h * 512, 512)
            s = scaled[pl.ds(r0, T1)]
            a = jnp.dot(s, we[:, pl.ds(c, 512)], preferred_element_type=F32)
            b = jax.nn.sigmoid(jnp.dot(s, we[:, pl.ds(D + c, 512)], preferred_element_type=F32))
            lin[pl.ds(r0, T1), pl.ds(c, 512)] = a
            gate[pl.ds(r0, T1), pl.ds(c, 512)] = b
            glu[pl.ds(pl.multiple_of(r0 + 16, 16), T1), pl.ds(c, 512)] = jnp.where(valid, a * b, 0.0).astype(BF16).astype(F32)

    glu[pl.ds(8, 8)] = glu[pl.ds(16 + FR + HALO, 8)]
    glu[pl.ds(0, 8)] = jnp.zeros((8, D), F32)

    @pl.loop(0, D // CC)
    def _(n):
        c = pl.ds(pl.multiple_of(n * CC, CC), CC)
        tap = [jnp.broadcast_to(taps[t : t + 1, c], (8, CC)) for t in range(KER)]

        @pl.loop(0, EXT // RC)
        def _(k):
            r0 = pl.multiple_of(k * RC, 16)
            wide = glu[pl.ds(r0, RC + 16), c]
            acc = None
            for t in range(KER):
                term = (wide[4 + t : 4 + t + RC].reshape(RC // 8, 8, CC) * tap[t]).reshape(RC, CC)
                acc = term if acc is None else acc + term
            dgrad[pl.ds(pl.multiple_of(r0 + 8, 8), RC), c] = acc

    def middle(depth, gs):
        normed, inverse = normalize(depth)
        sc = normed * conv_gain[...]
        sig = jax.nn.sigmoid(sc)
        sw = sc * sig
        gsc = gs * (sig + sw * (1.0 - sig))
        return norm_back(gsc * conv_gain[...], normed, inverse), sw, gsc * normed

    @pl.loop(0, FR // RT)
    def _(k):
        r0 = pl.multiple_of(k * RT, RT)
        at = pl.ds(pl.multiple_of(r0 + 16, 16), RT)
        gd, sw, gc = middle(dgrad[at], gsw[pl.ds(r0, RT)])
        dgrad[at] = gd
        swished[pl.ds(r0, RT)] = sw.astype(BF16)
        gainsum[0] += fold(gc)

    gd, _, _ = middle(
        jnp.concatenate([dgrad[8:16], dgrad[FR + 16 : FR + 24]], axis=0),
        jnp.concatenate([gsw[FR + HALO : EXT], gsw[FR : FR + HALO]], axis=0))
    dgrad[8:16] = gd[:8]
    dgrad[FR + 16 : FR + 24] = gd[8:]

    def view(p, s, c, cols):
        index = {"x": slice(None), "z": slice(None), "y": slice(None)}
        for a in ORDERS[p][:s]:
            index[a] = pos[a]
        index[ORDERS[p][s]] = lax.rem(c + 4, 4)
        return (p, index["x"], index["z"], index["y"], slice(None), cols)

    flying, pairs, done = {}, {}, []

    def pair_start(p):
        pairs[p] = pltpu.make_async_remote_copy(
            away.at[p], pair.at[p], pair_sem.at[0, p], pair_sem.at[1, p], device_id=partner, device_id_type=MESH)
        pairs[p].start()

    def pair_finish(p):
        pairs[p].wait_recv()

        @pl.loop(0, 16)
        def _(i):
            a, b = i // 4, lax.rem(i, 4)
            part[p, a, b] = (part[p, a, b].astype(F32) + pair[p, a, b].astype(F32)).astype(BF16)

    def step(p, s, n, at, dst, by):
        c = pltpu.make_async_remote_copy(
            part.at[at], dst, hop_send.at[p, s, n], hop_recv.at[p, s, n],
            device_id=along(ORDERS[p][s], by), device_id_type=MESH)
        c.start()
        flying[p, s].append(c)
        done.append(c)

    def ring_start(p, s):
        m = pos[ORDERS[p][s]]
        flying[p, s] = []
        step(p, s, 0, view(p, s, m + 2, LO), hop1[s].at[p, 0], 1)
        step(p, s, 1, view(p, s, m + 2, HI), hop1[s].at[p, 1], -1)
        step(p, s, 2, view(p, s, m + 1, HI), hop2[s].at[p, 0], 1)
        step(p, s, 3, view(p, s, m - 1, LO), hop2[s].at[p, 1], -1)

    def ring_middle(p, s):
        m = pos[ORDERS[p][s]]
        for n, (by, cols) in enumerate(((1, LO), (-1, HI))):
            flying[p, s][n].wait_recv()
            at = view(p, s, m + by, cols)
            part[at] = (part[at].astype(F32) + hop1[s][p, n].astype(F32)).astype(BF16)
            step(p, s, 4 + n, at, hop2[s].at[p, 2 + n], by)

    def ring_end(p, s):
        m = pos[ORDERS[p][s]]
        for c in flying[p, s][2:]:
            c.wait_recv()
        low, high = view(p, s, m, LO), view(p, s, m, HI)
        sum_low = part[low].astype(F32) + hop2[s][p, 2].astype(F32) + hop2[s][p, 1].astype(F32)
        sum_high = part[high].astype(F32) + hop2[s][p, 0].astype(F32) + hop2[s][p, 3].astype(F32)
        if s < 2:
            part[low] = sum_low.astype(BF16)
            part[high] = sum_high.astype(BF16)
        else:
            final[core, y, :, p * COLS : p * COLS + HALF] = sum_low.astype(BF16)
            final[core, y, :, p * COLS + HALF : (p + 1) * COLS] = sum_high.astype(BF16)

    small_flying = {}

    def small_start(s, value):
        axis = "xzy"[s]
        buf = ring_small.at[s]
        buf[pos[axis]] = value
        small_flying[s] = []
        for by in (1, 2, 3):
            c = pltpu.make_async_remote_copy(
                buf.at[pos[axis]], buf.at[pos[axis]], sm_sem.at[0, 3 * s + by], sm_sem.at[1, 3 * s + by],
                device_id=along(axis, by), device_id_type=MESH)
            c.start()
            small_flying[s].append(c)

    def small_end(s):
        for c in small_flying[s]:
            c.wait()
        b = ring_small.at[s]
        return (b[0] + b[1]) + (b[2] + b[3])

    def project_grad(dst, half):
        @pl.loop(0, 4)
        def _(k):
            value = contract_rows(
                swished[:, pl.ds(pl.multiple_of(k * 256, 256), 256)], cotv[:, pl.ds(pl.multiple_of(half * 512, 512), 512)])
            dst[0, k] = value.astype(BF16).reshape(4, 4, 16, COLS)

    project_grad(away, 1 - core)
    pair_start(0)
    project_grad(part, core)

    @pl.loop(0, 4)
    def _(k):
        r0 = pl.multiple_of(k * 256, 256)
        frame = r0 + lax.broadcasted_iota(jnp.int32, (256, 1), 0)
        projected = jnp.dot(swished[pl.ds(r0, 256)], wp[...], preferred_element_type=F32)
        swished[pl.ds(r0, 256)] = jnp.where(frame < live, seq[pl.ds(r0, 256)] + projected, 0.0).astype(BF16)

    put_out = pltpu.make_async_copy(swished, layer_out, local.at[4])
    put_out.start()
    pair_finish(0)
    ring_start(0, 0)

    def conv_back(lo, hi):
        @pl.loop(lo, hi)
        def _(n):
            c = pl.ds(pl.multiple_of(n * CC, CC), CC)
            tap = [jnp.broadcast_to(taps[t : t + 1, c], (8, CC)) for t in range(KER)]

            def rows(k, sums):
                r0 = pl.multiple_of(k * RB, RB)
                frame = r0 + lax.broadcasted_iota(jnp.int32, (RB, 1), 0)
                wide = dgrad[pl.ds(pl.multiple_of(r0 + 8, 8), RB + 16), c]
                mid = glu[pl.ds(pl.multiple_of(r0 + 16, 16), RB), c]
                acc, new = None, []
                for t in range(KER):
                    shifted = wide[12 - t : 12 - t + RB]
                    term = (shifted.reshape(RB // 8, 8, CC) * tap[t]).reshape(RB, CC)
                    acc = term if acc is None else acc + term
                    new.append(sums[t] + fold(mid * shifted))
                a = lin[pl.ds(r0, RB), c]
                b = gate[pl.ds(r0, RB), c]
                gg = jnp.where(frame < live, acc, 0.0) * b
                arrived[pl.ds(r0, RB), c] = gg.astype(BF16)
                arrived[pl.ds(pl.multiple_of(FR + r0, RB), RB), c] = (gg * a * (1.0 - b)).astype(BF16)
                return tuple(new)

            sums = lax.fori_loop(0, FR // RB, rows, tuple(jnp.zeros((8, CC), F32) for _ in range(KER)))
            for t in range(KER):
                small[t : t + 1, c] = jnp.sum(sums[t], axis=0, keepdims=True)

    conv_back(0, 4)
    ring_middle(0, 0)
    conv_back(4, 8)

    def expand_grad(dst, half):
        @pl.loop(0, 4)
        def _(k):
            value = contract_rows(
                scaled[pl.ds(0, FR), pl.ds(pl.multiple_of(k * 256, 256), 256)],
                arrived[pl.ds(pl.multiple_of(half * FR, FR), FR)]).astype(BF16)
            dst[1, k] = value[:, :COLS].reshape(4, 4, 16, COLS)
            dst[2, k] = value[:, COLS:].reshape(4, 4, 16, COLS)

    expand_grad(away, 1 - core)
    pair_start(1)
    pair_start(2)
    ring_end(0, 0)
    ring_start(0, 1)
    expand_grad(part, core)
    for p in (1, 2):
        pair_finish(p)
        ring_start(p, 0)
    ring_middle(0, 1)

    def input_grad(lo, hi):
        @pl.loop(lo, hi)
        def _(k):
            r0 = pl.multiple_of(k * 256, 256)
            grad_scaled = contract_cols(arrived[pl.ds(r0, 256)], we[:, :D]) + contract_cols(
                arrived[pl.ds(pl.multiple_of(FR + r0, 256), 256)], we[:, D:])
            normed, inverse = normalize(seq[pl.ds(r0, 256)])
            gainsum[1] += fold(grad_scaled * normed)
            cotv[pl.ds(r0, 256)] = (
                cotv[pl.ds(r0, 256)].astype(F32) + norm_back(grad_scaled * norm_gain[...], normed, inverse)
            ).astype(BF16)

    input_grad(0, 2)
    for p in (1, 2):
        ring_middle(p, 0)
    input_grad(2, 4)
    put_grad = pltpu.make_async_copy(cotv, grad_in, local.at[5])
    put_grad.start()
    small[9:10] = jnp.sum(gainsum[1], axis=0, keepdims=True)
    small[10:11] = jnp.sum(gainsum[0], axis=0, keepdims=True)
    there = pl.multiple_of((1 - core) * 512, 512)
    here = pl.multiple_of(core * 512, 512)
    small_pair = pltpu.make_async_remote_copy(
        small.at[:, pl.ds(there, 512)], pair_small, sm_sem.at[0, 0], sm_sem.at[1, 0], device_id=partner, device_id_type=MESH)
    small_pair.start()
    for p in (1, 2):
        ring_end(p, 0)
        ring_start(p, 1)
    ring_end(0, 1)
    ring_start(0, 2)
    small_pair.wait()
    small_start(0, small[:, pl.ds(here, 512)] + pair_small[...])
    for p in (1, 2):
        ring_middle(p, 1)
    ring_middle(0, 2)
    small_start(1, small_end(0))
    for p in (1, 2):
        ring_end(p, 1)
        ring_start(p, 2)
    ring_end(0, 2)
    for p in (1, 2):
        ring_middle(p, 2)
    small_start(2, small_end(1))
    for p in (1, 2):
        ring_end(p, 2)

    gather = []
    for by in (1, 2, 3):
        c = pltpu.make_async_remote_copy(
            final.at[core, y], final.at[core, y], fin_sem.at[0, by - 1], fin_sem.at[1, by - 1],
            device_id=along("y", by), device_id_type=MESH)
        c.start()
        gather.append(c)
    full_small[core] = small_end(2)
    small_last = pltpu.make_async_remote_copy(
        full_small.at[core], full_small.at[core], sm_sem.at[0, 10], sm_sem.at[1, 10], device_id=partner, device_id_type=MESH)
    small_last.start()
    for c in gather:
        c.wait_recv()
    final_last = pltpu.make_async_remote_copy(
        final.at[core], final.at[core], fin_sem.at[0, 3], fin_sem.at[1, 3], device_id=partner, device_id_type=MESH)
    final_last.start()
    for c in list(copies.values()) + gather + list(pairs.values()) + done:
        c.wait_send()
    put_out.wait()
    put_grad.wait()
    small_last.wait()
    out_small[:, 0:512] = full_small[0]
    out_small[:, 512:1024] = full_small[1]
    final_last.wait()
    out_sum[...] = final[...]


def finish_kernel(layer_in, grad_src, sums, small, layer_out, grad_in, expand, project, taps, norm_gain, conv_gain):
    layer_out[0] = layer_in[...]
    grad_in[0] = grad_src[...]

    @pl.when(pl.program_id(0) == 0)
    def _():
        for k in range(4):
            for c in range(2):
                rows = sums[c, k].astype(F32)
                project[k * 16 : k * 16 + 16, c * 512 : (c + 1) * 512] = rows[:, :512]
                expand[k * 16 : k * 16 + 16, c * 1024 : (c + 1) * 1024] = rows[:, 512:]
        taps[...] = small[0:KER]
        norm_gain[...] = small[9:10]
        conv_gain[...] = small[10:11]


def per_device(
    loader_rows, frame_counts, lengths, cotangent, norm_gain, w_expand, conv_taps, conv_gain, w_project,
):
    any_space = pl.BlockSpec(memory_space=pl.ANY)
    vmem = pl.BlockSpec(memory_space=pltpu.VMEM)
    smem = pl.BlockSpec(memory_space=pltpu.SMEM)

    def hop_shapes(n):
        return [pltpu.VMEM((3, n) + (4,) * (2 - s) + (16, HALF), BF16) for s in range(3)]

    layer_out, grad_in, _, sums, small = pl.pallas_call(
        kernel,
        out_shape=[
            jax.ShapeDtypeStruct((FR, D), BF16),
            jax.ShapeDtypeStruct((FR, D), BF16),
            jax.ShapeDtypeStruct((N_RELAY * PIECE, D), BF16),
            jax.ShapeDtypeStruct((2, 4, 16, 3 * COLS), BF16),
            jax.ShapeDtypeStruct((16, D), F32),
        ],
        in_specs=[any_space, any_space, smem, smem, vmem, any_space, vmem, vmem, any_space],
        out_specs=[any_space] * 3 + [vmem] * 2,
        scratch_shapes=[
            pltpu.VMEM((16 * CAP, D), BF16),
            pltpu.VMEM((FR, D), BF16),
            pltpu.VMEM((2, 16, D), BF16),
            pltpu.VMEM((D, D), BF16),
            pltpu.VMEM((D, 2 * D), BF16),
            pltpu.VMEM((EXT, D), F32),
            pltpu.VMEM((EXT, D), F32),
            pltpu.VMEM((FR + 32, D), F32),
            pltpu.VMEM((FR + 32, D), F32),
            pltpu.VMEM((EXT, D), F32),
            pltpu.VMEM((EXT, D), F32),
            pltpu.VMEM((EXT, D), BF16),
            pltpu.VMEM((FR, D), BF16),
            pltpu.VMEM((2, 8, D), F32),
            pltpu.VMEM((16, D), F32),
            pltpu.VMEM((3, 4, 4, 4, 16, COLS), BF16),
            pltpu.VMEM((3, 4, 4, 4, 16, COLS), BF16),
            pltpu.VMEM((3, 4, 4, 4, 16, COLS), BF16),
            *hop_shapes(2),
            *hop_shapes(4),
            pltpu.VMEM((2, 4, 16, 3 * COLS), BF16),
            pltpu.VMEM((16, 512), F32),
            pltpu.VMEM((3, 4, 16, 512), F32),
            pltpu.VMEM((2, 16, 512), F32),
            DMA((N_HOPS,)),
            DMA((N_HOPS,)),
            DMA((6,)),
            DMA((8,)),
            DMA((2, 3)),
            DMA((3, 3, 6)),
            DMA((3, 3, 6)),
            DMA((2, 4)),
            DMA((2, 11)),
        ],
        compiler_params=pltpu.CompilerParams(collective_id=0, has_side_effects=True, vmem_limit_bytes=VMEM_LIMIT),
    )(
        loader_rows[0], cotangent[0], frame_counts[0], lengths, norm_gain[None], w_expand, conv_taps, conv_gain[None],
        w_project,
    )
    layer_out, grad_in, expand, project, taps, norm_gain, conv_gain = pl.pallas_call(
        finish_kernel,
        out_shape=[
            jax.ShapeDtypeStruct((1, FR, D), BF16),
            jax.ShapeDtypeStruct((1, FR, D), BF16),
            jax.ShapeDtypeStruct((D // 16, 2 * D), F32),
            jax.ShapeDtypeStruct((D // 16, D), F32),
            jax.ShapeDtypeStruct((KER, D), F32),
            jax.ShapeDtypeStruct((1, D), F32),
            jax.ShapeDtypeStruct((1, D), F32),
        ],
        grid=(4,),
        in_specs=[pl.BlockSpec((FR // 4, D), lambda i: (i, 0))] * 2 + [vmem] * 2,
        out_specs=[pl.BlockSpec((1, FR // 4, D), lambda i: (0, i, 0))] * 2 + [vmem] * 5,
    )(layer_out, grad_in, sums, small)
    return layer_out, grad_in, expand, project, taps, norm_gain[0], conv_gain[0]


def solution(mesh):
    return jax.shard_map(
        per_device,
        mesh=mesh,
        in_specs=(
            P("rec", "tm", None), P("rec", None, None), P("rec"), P("rec", "tm", None),
            P(), P(), P(), P(), P(),
        ),
        out_specs=(
            P("rec", "tm", None), P("rec", "tm", None), P("tm", None), P("tm", None), P(), P(), P(),
        ),
        check_vma=False,
    )
```

```python
import functools

import jax
import jax.numpy as jnp
from jax import lax
from jax.experimental import pallas as pl
from jax.experimental.pallas import tpu as pltpu
from jax.sharding import PartitionSpec as P

EPS = 1e-05
MESH = pl.DeviceIdType.MESH
DMA = pltpu.SemaphoreType.DMA
F32 = jnp.float32
BF16 = jnp.bfloat16
D = 1024
FR = 1024
CAP = 128
KER = 9
HALO = 8
EXT = FR + 2 * HALO
VMEM_LIMIT = 61 * 1024 * 1024


def place():
    rec, tm = lax.axis_index("rec"), lax.axis_index("tm")
    return rec // 2, rec % 2, tm // 4, tm % 4


def device(y, core, x, z):
    return (lax.rem(y + 4, 4) * 2 + core, lax.rem(x + 4, 4) * 4 + lax.rem(z + 4, 4))


def greet(devices):
    barrier = pltpu.get_barrier_semaphore()
    for d in devices:
        pl.semaphore_signal(barrier, inc=1, device_id=d, device_id_type=MESH)
    pl.semaphore_wait(barrier, len(devices))


def contract_rows(left, right):
    return lax.dot_general(left, right, (((0,), (0,)), ((), ())), preferred_element_type=F32)


def contract_cols(left, right):
    return lax.dot_general(left, right, (((1,), (1,)), ((), ())), preferred_element_type=F32)


def row_frames(start, rows):
    row = start + lax.broadcasted_iota(jnp.int32, (rows, 1), 0)
    return jnp.where(row < FR + HALO, row, row - EXT)


OFFSETS = [(dx, dz) for dx in range(4) for dz in range(4) if (dx, dz) != (0, 0)]
SIGNED = (0, 1, None, -1)


def routes():
    out = []
    for dx, dz in OFFSETS:
        for half in (0, 1):
            sign_x = (1 - 2 * half) * (-1 if dz == 3 else 1)
            sign_z = (1 - 2 * half) * (-1 if dx == 1 else 1)
            step_x = sign_x if dx == 2 else SIGNED[dx]
            step_z = sign_z if dz == 2 else SIGNED[dz]
            along_x = [(step_x, 0)] * (0 if dx == 0 else 2 if dx == 2 else 1)
            along_z = [(0, step_z)] * (0 if dz == 0 else 2 if dz == 2 else 1)
            hops = along_x + along_z if half == 0 else along_z + along_x
            out.append(((dx, dz), half, hops))
    return sorted(out, key=lambda r: -len(r[2]))


ROUTES = routes()
N_HOPS = sum(len(r[2]) for r in ROUTES)
N_RELAY = sum(len(r[2]) - 1 for r in ROUTES)
PIECE = CAP // 2


def mean(values):
    return jnp.mean(values, axis=-1, keepdims=True)


def lanes(n):
    return slice(n * CC, (n + 1) * CC)


def spread(values):
    return jnp.broadcast_to(mean(values) * (CC / D), values.shape)


def moments(load):
    center = spread(sum(load(n) for n in range(D // CC)))
    square = None
    for n in range(D // CC):
        off = load(n) - center
        square = off * off if square is None else square + off * off
    return center, lax.rsqrt(spread(square) + EPS)


def fold(values):
    return jnp.sum(values.reshape(-1, 8, values.shape[-1]), axis=0)


T1 = 208
RM = 128
RC = 208
RB = 128
RT = 64
CC = 128


ORDERS = (("z", "x"), ("x", "z"), ("z", "x"))
WIDTH = (512, 768, 256)
START = (0, 512, 1280)


def kernel(
    loader, cot, counts, length, norm_gain, w_expand, taps, conv_gain, w_project,
    layer_out, grad_in, relay, out_sum, out_small,
    arrived, cotv, edge, wp, we, seq, gsw, glu, dgrad, lin, gate, scaled, swished, gainsum, small, total, mean_in, inverse_in,
    away, pair, part, hop1, hop2, cross, tall, final, pair_small, ring_small, full_small,
    send, recv, local, edge_sem, pair_sem, hop_sem, cross_sem, tall_sem, fin_sem, sm_sem,
):
    y, core, x, z = place()
    pos = {"x": x, "y": y, "z": z}
    me = x * 4 + z
    live = length[0] - me * FR
    partner = device(y, 1 - core, x, z)

    def along(axis, by):
        at = dict(pos)
        at[axis] = pos[axis] + by
        return device(at["y"], core, at["x"], at["z"])

    greet([device(y, core, x + dx, z + dz) for dx, dz in OFFSETS] + [partner] + [along("y", b) for b in (1, 2, 3)])

    hop_id, slot = {}, {}
    for i, (_, _, hops) in enumerate(ROUTES):
        for k in range(len(hops)):
            hop_id[i, k] = len(hop_id)
            if k < len(hops) - 1:
                slot[i, k] = len(slot)
    copies = {}

    def launch(i, k, src):
        _, half, hops = ROUTES[i]
        gone_x, gone_z = (sum(h[a] for h in hops[:k]) for a in (0, 1))
        if k == len(hops) - 1:
            origin = lax.rem(x - gone_x + 4, 4) * 4 + lax.rem(z - gone_z + 4, 4)
            dst = arrived.at[pl.ds(origin * CAP + half * PIECE, PIECE)]
        else:
            dst = relay.at[pl.ds(slot[i, k] * PIECE, PIECE)]
        j = hop_id[i, k]
        copies[i, k] = pltpu.make_async_remote_copy(
            src, dst, send.at[j], recv.at[j],
            device_id=device(y, core, x + hops[k][0], z + hops[k][1]), device_id_type=MESH,
        )
        copies[i, k].start()

    before, after = lax.rem(me + 15, 16), lax.rem(me + 1, 16)
    left = device(y, core, before // 4, lax.rem(before, 4))
    right = device(y, core, after // 4, lax.rem(after, 4))
    first = pltpu.make_async_remote_copy(
        cot.at[pl.ds(0, 16)], edge.at[0], edge_sem.at[0], edge_sem.at[1], device_id=left, device_id_type=MESH)
    last = pltpu.make_async_remote_copy(
        cot.at[pl.ds(FR - 16, 16)], edge.at[1], edge_sem.at[2], edge_sem.at[3], device_id=right, device_id_type=MESH)
    first.start()
    last.start()
    for i, ((dx, dz), half, _) in enumerate(ROUTES):
        to = lax.rem(x + dx, 4) * 4 + lax.rem(z + dz, 4)
        launch(i, 0, loader.at[pl.ds(to * CAP + half * PIECE, PIECE)])
    own = pltpu.make_async_copy(loader.at[pl.ds(me * CAP, CAP)], arrived.at[pl.ds(me * CAP, CAP)], local.at[0])
    get_cot = pltpu.make_async_copy(cot, cotv, local.at[1])
    get_wp = pltpu.make_async_copy(w_project, wp, local.at[2])
    get_we = pltpu.make_async_copy(w_expand, we, local.at[3])
    for c in (get_cot, get_wp, own, get_we):
        c.start()
    get_cot.wait()
    get_wp.wait()

    @pl.loop(0, 4)
    def _(k):
        r0 = pl.multiple_of(k * 256, 256)
        frame = r0 + lax.broadcasted_iota(jnp.int32, (256, 1), 0)
        tile = cotv[pl.ds(r0, 256)]
        tile = jnp.where(frame < live, tile, jnp.zeros_like(tile))
        cotv[pl.ds(r0, 256)] = tile
        gsw[pl.ds(pl.multiple_of(r0 + 16, 16), 256)] = contract_cols(tile, wp[...])

    gainsum[...] = jnp.zeros_like(gainsum)
    total[...] = jnp.zeros_like(total)
    small[...] = jnp.zeros_like(small)

    column = [counts[j, me] for j in range(16)]
    lane = lax.broadcasted_iota(jnp.int32, (1, CAP), 1)

    def collect(offsets, fresh):
        origins, places = [], []
        for dx, dz in offsets:
            origin = lax.rem(x - dx + 4, 4) * 4 + lax.rem(z - dz + 4, 4)
            begin = count = jnp.int32(0)
            for j in range(16):
                begin = begin + jnp.where(j < origin, column[j], 0)
                count = count + jnp.where(j == origin, column[j], 0)
            origins.append(origin)
            places.append(jnp.where(lane < count, begin + lane, -1))
        places = jnp.concatenate(places, axis=1)

        @pl.loop(0, 4)
        def _(k):
            r0 = pl.multiple_of(k * 256, 256)
            frame = r0 + lax.broadcasted_iota(jnp.int32, (256, 1), 0)
            pick = jnp.where(frame == places, 1.0, 0.0).astype(BF16)
            rows = jnp.concatenate([arrived[pl.ds(pl.multiple_of(o * CAP, CAP), CAP)] for o in origins], axis=0)
            got = jnp.dot(pick, rows, preferred_element_type=F32)
            seq[pl.ds(r0, 256)] = got if fresh else seq[pl.ds(r0, 256)] + got

    def forward(k):
        for i, (_, _, hops) in enumerate(ROUTES):
            if k < len(hops):
                copies[i, k - 1].wait_recv()
                launch(i, k, relay.at[pl.ds(slot[i, k - 1] * PIECE, PIECE)])

    def arrive(steps, more, fresh):
        here = list(more)
        for i, (offset, _, hops) in enumerate(ROUTES):
            if len(hops) == steps:
                copies[i, steps - 1].wait_recv()
                if offset not in here:
                    here.append(offset)
        collect(here, fresh)

    forward(1)
    first.wait()
    last.wait()
    rim = jnp.concatenate([edge[0].astype(F32)[:HALO], edge[1].astype(F32)[16 - HALO :]], axis=0)
    frame = row_frames(FR, 2 * HALO)
    rim = jnp.where((frame < live) & (frame + me * FR >= 0), rim, 0.0).astype(BF16)
    rim = contract_cols(rim, wp[...])
    gsw[FR + 16 : FR + 24] = rim[:HALO]
    gsw[8:16] = rim[HALO:]
    own.wait()
    arrive(1, [(0, 0)], True)
    forward(2)
    arrive(2, [], False)
    forward(3)
    arrive(3, [], False)
    arrive(4, [], False)

    first = pltpu.make_async_remote_copy(
        seq.at[pl.ds(0, HALO)], seq.at[pl.ds(FR, HALO)], edge_sem.at[4], edge_sem.at[5], device_id=left, device_id_type=MESH)
    last = pltpu.make_async_remote_copy(
        seq.at[pl.ds(FR - HALO, HALO)], seq.at[pl.ds(FR + HALO, HALO)], edge_sem.at[6], edge_sem.at[7], device_id=right, device_id_type=MESH)
    first.start()
    last.start()
    get_we.wait()

    @pl.loop(0, EXT // T1)
    def _(k):
        @pl.when(k == EXT // T1 - 1)
        def _():
            first.wait()
            last.wait()

        r0 = pl.multiple_of(k * T1, 16)
        at = pl.ds(r0, T1)
        center, inverse = moments(lambda n: seq[at, lanes(n)])
        mean_in[at], inverse_in[at] = center, inverse
        for n in range(D // CC):
            scaled[at, lanes(n)] = ((seq[at, lanes(n)] - center) * inverse * norm_gain[:, lanes(n)]).astype(BF16)
        frame = row_frames(r0, T1)
        valid = (frame < live) & (frame + me * FR >= 0)

        @pl.loop(0, 2)
        def _(h):
            c = pl.multiple_of(h * 512, 512)
            s = scaled[pl.ds(r0, T1)]
            a = jnp.dot(s, we[:, pl.ds(c, 512)], preferred_element_type=F32)
            b = jax.nn.sigmoid(jnp.dot(s, we[:, pl.ds(D + c, 512)], preferred_element_type=F32))
            lin[pl.ds(r0, T1), pl.ds(c, 512)] = a
            gate[pl.ds(r0, T1), pl.ds(c, 512)] = b
            glu[pl.ds(pl.multiple_of(r0 + 16, 16), T1), pl.ds(c, 512)] = jnp.where(valid, a * b, 0.0).astype(BF16).astype(F32)

    glu[pl.ds(8, 8)] = glu[pl.ds(16 + FR + HALO, 8)]
    glu[pl.ds(0, 8)] = jnp.zeros((8, D), F32)

    @pl.loop(0, D // CC)
    def _(n):
        c = pl.ds(pl.multiple_of(n * CC, CC), CC)
        tap = [jnp.broadcast_to(taps[t : t + 1, c], (8, CC)) for t in range(KER)]

        @pl.loop(0, EXT // RC)
        def _(k):
            r0 = pl.multiple_of(k * RC, 16)
            wide = glu[pl.ds(r0, RC + 16), c]
            acc = None
            for t in range(KER):
                term = (wide[4 + t : 4 + t + RC].reshape(RC // 8, 8, CC) * tap[t]).reshape(RC, CC)
                acc = term if acc is None else acc + term
            at = pl.ds(pl.multiple_of(r0 + 8, 8), RC)
            dgrad[at, c] = acc
            total[at] += acc

    def middle(at, rows):
        center = spread(total[at])
        square = None
        for n in range(D // CC):
            off = dgrad[at, lanes(n)] - center
            square = off * off if square is None else square + off * off
        inverse = lax.rsqrt(spread(square) + EPS)
        sum_h = sum_hn = None
        for n in range(D // CC):
            gain = conv_gain[:, lanes(n)]
            normed = (dgrad[at, lanes(n)] - center) * inverse
            sc = normed * gain
            sig = jax.nn.sigmoid(sc)
            sw = sc * sig
            gsc = gsw[at, lanes(n)] * (sig + sw * (1.0 - sig))
            h = gsc * gain
            hn = h * normed
            gsw[at, lanes(n)] = h
            dgrad[at, lanes(n)] = normed
            sum_h = h if sum_h is None else sum_h + h
            sum_hn = hn if sum_hn is None else sum_hn + hn
            if rows is not None:
                swished[rows, lanes(n)] = sw.astype(BF16)
                gainsum[0, :, lanes(n)] += fold(gsc * normed)
        sum_h, sum_hn = spread(sum_h), spread(sum_hn)
        for n in range(D // CC):
            dgrad[at, lanes(n)] = inverse * (gsw[at, lanes(n)] - sum_h - dgrad[at, lanes(n)] * sum_hn)

    @pl.loop(0, FR // RM)
    def _(k):
        r0 = pl.multiple_of(k * RM, RM)
        middle(pl.ds(pl.multiple_of(r0 + 16, 16), RM), pl.ds(r0, RM))

    middle(slice(8, 16), None)
    middle(slice(FR + 16, FR + 24), None)

    def block(p, c, cols):
        c = lax.rem(c + 4, 4)
        index = (c, slice(None)) if ORDERS[p][0] == "x" else (slice(None), c)
        return index + (slice(None), slice(None), cols)

    def cell(p, c):
        c = lax.rem(c + 4, 4)
        return (x, c) if ORDERS[p][0] == "x" else (c, z)

    def low_high(p):
        return pl.ds(0, WIDTH[p] // 2), pl.ds(WIDTH[p] // 2, WIDTH[p] // 2)

    flying, crossing, climbing, pairs, finals, done = {}, {}, {}, {}, {}, []

    def pair_start(p):
        pairs[p] = pltpu.make_async_remote_copy(
            away[p], pair[p], pair_sem.at[0, p], pair_sem.at[1, p], device_id=partner, device_id_type=MESH)
        pairs[p].start()

    def pair_finish(p):
        pairs[p].wait_recv()

        @pl.loop(0, 16)
        def _(i):
            a, b = i // 4, lax.rem(i, 4)
            part[p][a, b] = (part[p][a, b].astype(F32) + pair[p][a, b].astype(F32)).astype(BF16)

    def step(p, n, at, dst, by):
        c = pltpu.make_async_remote_copy(
            part[p].at[at], dst, hop_sem.at[0, p, n], hop_sem.at[1, p, n],
            device_id=along(ORDERS[p][0], by), device_id_type=MESH)
        c.start()
        flying[p].append(c)
        done.append(c)

    def ring_start(p):
        m = pos[ORDERS[p][0]]
        lo, hi = low_high(p)
        flying[p] = []
        step(p, 0, block(p, m + 2, lo), hop1[p].at[0], 1)
        step(p, 1, block(p, m + 2, hi), hop1[p].at[1], -1)
        step(p, 2, block(p, m + 1, hi), hop2[p].at[0], 1)
        step(p, 3, block(p, m - 1, lo), hop2[p].at[1], -1)

    def ring_middle(p):
        m = pos[ORDERS[p][0]]
        for n, (by, cols) in enumerate(zip((1, -1), low_high(p))):
            flying[p][n].wait_recv()
            at = block(p, m + by, cols)
            part[p][at] = (part[p][at].astype(F32) + hop1[p][n].astype(F32)).astype(BF16)
            step(p, 4 + n, at, hop2[p].at[2 + n], by)

    def ring_end(p):
        m = pos[ORDERS[p][0]]
        for c in flying[p][2:]:
            c.wait_recv()
        low, high = (block(p, m, cols) for cols in low_high(p))
        part[p][low] = (part[p][low].astype(F32) + hop2[p][2].astype(F32) + hop2[p][1].astype(F32)).astype(BF16)
        part[p][high] = (part[p][high].astype(F32) + hop2[p][0].astype(F32) + hop2[p][3].astype(F32)).astype(BF16)
        crossing[p] = []
        for by in (2, 1, 3):
            c = pltpu.make_async_remote_copy(
                part[p].at[cell(p, pos[ORDERS[p][1]] + by)], cross[p].at[by - 1], cross_sem.at[0, p, by - 1], cross_sem.at[1, p, by - 1],
                device_id=along(ORDERS[p][1], by), device_id_type=MESH)
            c.start()
            crossing[p].append(c)
            done.append(c)

    def cross_end(p):
        for c in crossing[p]:
            c.wait_recv()
        total_here = part[p][cell(p, pos[ORDERS[p][1]])].astype(F32)
        for k in range(3):
            total_here = total_here + cross[p][k].astype(F32)
        tall[p][y] = total_here.astype(BF16)
        climbing[p] = []
        for by in (2, 1, 3):
            c = pltpu.make_async_remote_copy(
                tall[p].at[y], tall[p].at[y], tall_sem.at[0, p, by - 1], tall_sem.at[1, p, by - 1],
                device_id=along("y", by), device_id_type=MESH)
            c.start()
            climbing[p].append(c)
            done.append(c)

    def tall_end(p):
        for c in climbing[p]:
            c.wait_recv()
        t = [tall[p][k].astype(F32) for k in range(4)]
        mine = final.at[core, :, :, START[p] : START[p] + WIDTH[p]]
        mine[...] = (t[0] + t[1]) + (t[2] + t[3])
        finals[p] = pltpu.make_async_remote_copy(
            mine, mine, fin_sem.at[0, p], fin_sem.at[1, p], device_id=partner, device_id_type=MESH)
        finals[p].start()

    small_flying = {}

    def small_start(s, value):
        axis = "xzy"[s]
        buf = ring_small.at[s]
        buf[pos[axis]] = value
        small_flying[s] = []
        for by in (1, 2, 3):
            c = pltpu.make_async_remote_copy(
                buf.at[pos[axis]], buf.at[pos[axis]], sm_sem.at[0, 3 * s + by], sm_sem.at[1, 3 * s + by],
                device_id=along(axis, by), device_id_type=MESH)
            c.start()
            small_flying[s].append(c)

    def small_end(s):
        for c in small_flying[s]:
            c.wait()
        b = ring_small.at[s]
        return (b[0] + b[1]) + (b[2] + b[3])

    def project_grad(dst, half):
        @pl.loop(0, 4)
        def _(k):
            value = contract_rows(
                swished[:, pl.ds(pl.multiple_of(k * 256, 256), 256)], cotv[:, pl.ds(pl.multiple_of(half * 512, 512), 512)])
            dst[0][k] = value.astype(BF16).reshape(4, 4, 16, WIDTH[0])

    project_grad(away, 1 - core)
    pair_start(0)
    project_grad(part, core)

    def project(lo, hi):
        @pl.loop(lo, hi)
        def _(k):
            r0 = pl.multiple_of(k * 256, 256)
            frame = r0 + lax.broadcasted_iota(jnp.int32, (256, 1), 0)
            projected = jnp.dot(swished[pl.ds(r0, 256)], wp[...], preferred_element_type=F32)
            swished[pl.ds(r0, 256)] = jnp.where(frame < live, seq[pl.ds(r0, 256)] + projected, 0.0).astype(BF16)

    pair_finish(0)
    ring_start(0)

    def conv_back(lo, hi):
        @pl.loop(lo, hi)
        def _(n):
            c = pl.ds(pl.multiple_of(n * CC, CC), CC)
            tap = [jnp.broadcast_to(taps[t : t + 1, c], (8, CC)) for t in range(KER)]

            def rows(k, sums):
                r0 = pl.multiple_of(k * RB, RB)
                frame = r0 + lax.broadcasted_iota(jnp.int32, (RB, 1), 0)
                wide = dgrad[pl.ds(pl.multiple_of(r0 + 8, 8), RB + 16), c]
                mid = glu[pl.ds(pl.multiple_of(r0 + 16, 16), RB), c]
                acc, new = None, []
                for t in range(KER):
                    shifted = wide[12 - t : 12 - t + RB]
                    term = (shifted.reshape(RB // 8, 8, CC) * tap[t]).reshape(RB, CC)
                    acc = term if acc is None else acc + term
                    new.append(sums[t] + fold(mid * shifted))
                a = lin[pl.ds(r0, RB), c]
                b = gate[pl.ds(r0, RB), c]
                gg = jnp.where(frame < live, acc, 0.0) * b
                arrived[pl.ds(r0, RB), c] = gg.astype(BF16)
                arrived[pl.ds(pl.multiple_of(FR + r0, RB), RB), c] = (gg * a * (1.0 - b)).astype(BF16)
                return tuple(new)

            sums = lax.fori_loop(0, FR // RB, rows, tuple(jnp.zeros((8, CC), F32) for _ in range(KER)))
            for t in range(KER):
                small[t : t + 1, c] = jnp.sum(sums[t], axis=0, keepdims=True)

    def expand_grad(dst, p, half):
        first_col = START[p] - START[1]

        @pl.loop(0, 4)
        def _(k):
            value = contract_rows(
                scaled[pl.ds(0, FR), pl.ds(pl.multiple_of(k * 256, 256), 256)],
                arrived[pl.ds(pl.multiple_of(half * FR, FR), FR), first_col : first_col + WIDTH[p]])
            dst[p][k] = value.astype(BF16).reshape(4, 4, 16, WIDTH[p])

    conv_back(0, 3)
    ring_middle(0)
    conv_back(3, 6)
    expand_grad(away, 1, 1 - core)
    pair_start(1)
    ring_end(0)
    expand_grad(part, 1, core)
    conv_back(6, 8)
    pair_finish(1)
    ring_start(1)
    expand_grad(away, 2, 1 - core)
    pair_start(2)
    cross_end(0)
    expand_grad(part, 2, core)
    pair_finish(2)
    ring_start(2)
    tall_end(0)

    def input_grad(lo, hi):
        @pl.loop(lo, hi)
        def _(k):
            r0 = pl.multiple_of(k * 256, 256)
            grad_scaled = contract_cols(arrived[pl.ds(r0, 256)], we[:, :D]) + contract_cols(
                arrived[pl.ds(pl.multiple_of(FR + r0, 256), 256)], we[:, D:])
            at = pl.ds(r0, 256)
            gsw[at] = grad_scaled
            center, inverse = mean_in[at], inverse_in[at]
            sum_g = sum_gn = None
            for n in range(D // CC):
                normed = (seq[at, lanes(n)] - center) * inverse
                product = gsw[at, lanes(n)] * normed
                gainsum[1, :, lanes(n)] += fold(product)
                g = gsw[at, lanes(n)] * norm_gain[:, lanes(n)]
                gn = product * norm_gain[:, lanes(n)]
                sum_g = g if sum_g is None else sum_g + g
                sum_gn = gn if sum_gn is None else sum_gn + gn
            sum_g, sum_gn = spread(sum_g), spread(sum_gn)
            for n in range(D // CC):
                normed = (seq[at, lanes(n)] - center) * inverse
                g = gsw[at, lanes(n)] * norm_gain[:, lanes(n)]
                cotv[at, lanes(n)] = (
                    cotv[at, lanes(n)].astype(F32) + inverse * (g - sum_g - normed * sum_gn)).astype(BF16)

    input_grad(0, 2)
    ring_middle(1)
    ring_middle(2)
    input_grad(2, 4)
    put_grad = pltpu.make_async_copy(cotv, grad_in, local.at[5])
    put_grad.start()
    small[9:10] = jnp.sum(gainsum[1], axis=0, keepdims=True)
    small[10:11] = jnp.sum(gainsum[0], axis=0, keepdims=True)
    there = pl.multiple_of((1 - core) * 512, 512)
    here = pl.multiple_of(core * 512, 512)
    small_pair = pltpu.make_async_remote_copy(
        small.at[:, pl.ds(there, 512)], pair_small, sm_sem.at[0, 0], sm_sem.at[1, 0], device_id=partner, device_id_type=MESH)
    small_pair.start()
    ring_end(2)
    small_pair.wait()
    small_start(0, small[:, pl.ds(here, 512)] + pair_small[...])
    ring_end(1)
    project(0, 2)
    cross_end(2)
    small_start(1, small_end(0))
    project(2, 4)
    put_out = pltpu.make_async_copy(swished, layer_out, local.at[4])
    put_out.start()
    cross_end(1)
    small_start(2, small_end(1))
    tall_end(2)
    tall_end(1)
    full_small[core] = small_end(2)
    small_last = pltpu.make_async_remote_copy(
        full_small.at[core], full_small.at[core], sm_sem.at[0, 10], sm_sem.at[1, 10], device_id=partner, device_id_type=MESH)
    small_last.start()
    for c in list(copies.values()) + list(pairs.values()) + done:
        c.wait_send()
    put_out.wait()
    put_grad.wait()
    small_last.wait()
    out_small[:, 0:512] = full_small[0]
    out_small[:, 512:1024] = full_small[1]
    for c in finals.values():
        c.wait()
    out_sum[...] = final[...]


def finish_kernel(
    layer_in, grad_src, sums, small, layer_out, grad_in, expand, project, taps, norm_gain, conv_gain, rows, get_sem, put_sem,
):
    gets, puts = [], []
    for i, src in enumerate((layer_in, grad_src)):
        for k in range(4):
            at = pl.ds(k * 256, 256)
            c = pltpu.make_async_copy(src.at[at], rows.at[i, at], get_sem.at[i, k])
            c.start()
            gets.append((i, k, c))
    for k in range(4):
        for c in range(2):
            values = sums[c, k]
            project[k * 16 : k * 16 + 16, c * 512 : (c + 1) * 512] = values[:, :512]
            expand[k * 16 : k * 16 + 16, c * 1024 : (c + 1) * 1024] = values[:, 512:]
    taps[...] = small[0:KER]
    norm_gain[...] = small[9:10]
    conv_gain[...] = small[10:11]
    for i, k, c in gets:
        c.wait()
        at = pl.ds(k * 256, 256)
        put = pltpu.make_async_copy(rows.at[i, at], (layer_out, grad_in)[i].at[0, at], put_sem.at[i, k])
        put.start()
        puts.append(put)
    for put in puts:
        put.wait()


def per_device(
    loader_rows, frame_counts, lengths, cotangent, norm_gain, w_expand, conv_taps, conv_gain, w_project,
):
    any_space = pl.BlockSpec(memory_space=pl.ANY)
    vmem = pl.BlockSpec(memory_space=pltpu.VMEM)
    smem = pl.BlockSpec(memory_space=pltpu.SMEM)

    def each(shape_of):
        return tuple(pltpu.VMEM(shape_of(w), BF16) for w in WIDTH)

    layer_out, grad_in, _, sums, small = pl.pallas_call(
        kernel,
        out_shape=[
            jax.ShapeDtypeStruct((FR, D), BF16),
            jax.ShapeDtypeStruct((FR, D), BF16),
            jax.ShapeDtypeStruct((N_RELAY * PIECE, D), BF16),
            jax.ShapeDtypeStruct((2, 4, 16, sum(WIDTH)), F32),
            jax.ShapeDtypeStruct((16, D), F32),
        ],
        in_specs=[any_space, any_space, smem, smem, vmem, any_space, vmem, vmem, any_space],
        out_specs=[any_space] * 3 + [vmem] * 2,
        scratch_shapes=[
            pltpu.VMEM((16 * CAP, D), BF16),
            pltpu.VMEM((FR, D), BF16),
            pltpu.VMEM((2, 16, D), BF16),
            pltpu.VMEM((D, D), BF16),
            pltpu.VMEM((D, 2 * D), BF16),
            pltpu.VMEM((EXT, D), F32),
            pltpu.VMEM((FR + 32, D), F32),
            pltpu.VMEM((FR + 32, D), F32),
            pltpu.VMEM((FR + 32, D), F32),
            pltpu.VMEM((EXT, D), F32),
            pltpu.VMEM((EXT, D), F32),
            pltpu.VMEM((EXT, D), BF16),
            pltpu.VMEM((FR, D), BF16),
            pltpu.VMEM((2, 8, D), F32),
            pltpu.VMEM((16, D), F32),
            pltpu.VMEM((FR + 32, CC), F32),
            pltpu.VMEM((EXT, CC), F32),
            pltpu.VMEM((EXT, CC), F32),
            *[each(lambda w: (4, 4, 4, 16, w)) for _ in range(3)],
            each(lambda w: (2, 4, 4, 16, w // 2)),
            each(lambda w: (4, 4, 4, 16, w // 2)),
            each(lambda w: (3, 4, 16, w)),
            each(lambda w: (4, 4, 16, w)),
            pltpu.VMEM((2, 4, 16, sum(WIDTH)), F32),
            pltpu.VMEM((16, 512), F32),
            pltpu.VMEM((3, 4, 16, 512), F32),
            pltpu.VMEM((2, 16, 512), F32),
            DMA((N_HOPS,)),
            DMA((N_HOPS,)),
            DMA((6,)),
            DMA((8,)),
            DMA((2, 3)),
            DMA((2, 3, 6)),
            DMA((2, 3, 3)),
            DMA((2, 3, 3)),
            DMA((2, 3)),
            DMA((2, 11)),
        ],
        compiler_params=pltpu.CompilerParams(collective_id=0, has_side_effects=True, vmem_limit_bytes=VMEM_LIMIT),
    )(
        loader_rows[0], cotangent[0], frame_counts[0], lengths, norm_gain[None], w_expand, conv_taps, conv_gain[None],
        w_project,
    )
    layer_out, grad_in, expand, project, taps, norm_gain, conv_gain = pl.pallas_call(
        finish_kernel,
        out_shape=[
            jax.ShapeDtypeStruct((1, FR, D), BF16),
            jax.ShapeDtypeStruct((1, FR, D), BF16),
            jax.ShapeDtypeStruct((D // 16, 2 * D), F32),
            jax.ShapeDtypeStruct((D // 16, D), F32),
            jax.ShapeDtypeStruct((KER, D), F32),
            jax.ShapeDtypeStruct((1, D), F32),
            jax.ShapeDtypeStruct((1, D), F32),
        ],
        in_specs=[any_space] * 2 + [vmem] * 2,
        out_specs=[any_space] * 2 + [vmem] * 5,
        scratch_shapes=[pltpu.VMEM((2, FR, D), BF16), DMA((2, 4)), DMA((2, 4))],
        compiler_params=pltpu.CompilerParams(vmem_limit_bytes=VMEM_LIMIT),
    )(layer_out, grad_in, sums, small)
    return layer_out, grad_in, expand, project, taps, norm_gain[0], conv_gain[0]


def solution(mesh):
    return jax.shard_map(
        per_device,
        mesh=mesh,
        in_specs=(
            P("rec", "tm", None), P("rec", None, None), P("rec"), P("rec", "tm", None),
            P(), P(), P(), P(), P(),
        ),
        out_specs=(
            P("rec", "tm", None), P("rec", "tm", None), P("tm", None), P("tm", None), P(), P(), P(),
        ),
        check_vma=False,
    )
```

```python
import functools

import jax
import jax.numpy as jnp
from jax import lax
from jax.experimental import pallas as pl
from jax.experimental.pallas import tpu as pltpu
from jax.sharding import PartitionSpec as P

EPS = 1e-05
MESH = pl.DeviceIdType.MESH
DMA = pltpu.SemaphoreType.DMA
F32 = jnp.float32
BF16 = jnp.bfloat16
D = 1024
FR = 1024
CAP = 128
KER = 9
HALO = 8
EXT = FR + 2 * HALO
VMEM_LIMIT = 61 * 1024 * 1024


def place():
    rec, tm = lax.axis_index("rec"), lax.axis_index("tm")
    return rec // 2, rec % 2, tm // 4, tm % 4


def device(y, core, x, z):
    return (lax.rem(y + 4, 4) * 2 + core, lax.rem(x + 4, 4) * 4 + lax.rem(z + 4, 4))


def greet(devices):
    barrier = pltpu.get_barrier_semaphore()
    for d in devices:
        pl.semaphore_signal(barrier, inc=1, device_id=d, device_id_type=MESH)
    pl.semaphore_wait(barrier, len(devices))


def contract_rows(left, right):
    return lax.dot_general(left, right, (((0,), (0,)), ((), ())), preferred_element_type=F32)


def contract_cols(left, right):
    return lax.dot_general(left, right, (((1,), (1,)), ((), ())), preferred_element_type=F32)


def row_frames(start, rows):
    row = start + lax.broadcasted_iota(jnp.int32, (rows, 1), 0)
    return jnp.where(row < FR + HALO, row, row - EXT)


OFFSETS = [(dx, dz) for dx in range(4) for dz in range(4) if (dx, dz) != (0, 0)]
SIGNED = (0, 1, None, -1)


def routes():
    out = []
    for dx, dz in OFFSETS:
        for half in (0, 1):
            sign_x = (1 - 2 * half) * (-1 if dz == 3 else 1)
            sign_z = (1 - 2 * half) * (-1 if dx == 1 else 1)
            step_x = sign_x if dx == 2 else SIGNED[dx]
            step_z = sign_z if dz == 2 else SIGNED[dz]
            along_x = [(step_x, 0)] * (0 if dx == 0 else 2 if dx == 2 else 1)
            along_z = [(0, step_z)] * (0 if dz == 0 else 2 if dz == 2 else 1)
            hops = along_x + along_z if half == 0 else along_z + along_x
            out.append(((dx, dz), half, hops))
    return sorted(out, key=lambda r: -len(r[2]))


ROUTES = routes()
N_HOPS = sum(len(r[2]) for r in ROUTES)
N_RELAY = sum(len(r[2]) - 1 for r in ROUTES)
PIECE = CAP // 2


def mean(values):
    return jnp.mean(values, axis=-1, keepdims=True)


def lanes(n):
    return slice(n * CC, (n + 1) * CC)


def spread(values):
    return jnp.broadcast_to(mean(values) * (CC / D), values.shape)


def moments(load):
    center = spread(sum(load(n) for n in range(D // CC)))
    square = None
    for n in range(D // CC):
        off = load(n) - center
        square = off * off if square is None else square + off * off
    return center, lax.rsqrt(spread(square) + EPS)


def fold(values):
    return jnp.sum(values.reshape(-1, 8, values.shape[-1]), axis=0)


T1 = 208
RM = 128
RC = 208
RB = 128
RT = 64
CC = 128


ORDERS = (("z", "x"), ("x", "z"), ("z", "x"))
WIDTH = (512, 768, 256)
START = (0, 512, 1280)


def kernel(
    loader, cot, counts, length, norm_gain_in, w_expand, taps_in, conv_gain_in, w_project,
    layer_out, grad_in, relay, out_sum, out_small,
    arrived, cotv, edge, wp, we, seq, gsw, glu, dgrad, lin, gate, scaled, swished, gainsum, small, total, mean_in, inverse_in, norm_gain, taps, conv_gain,
    away, pair, part, hop1, hop2, cross, tall, final, pair_small, ring_small, full_small,
    send, recv, local, edge_sem, pair_sem, hop_sem, cross_sem, tall_sem, fin_sem, sm_sem,
):
    y, core, x, z = place()
    pos = {"x": x, "y": y, "z": z}
    me = x * 4 + z
    live = length[0] - me * FR
    partner = device(y, 1 - core, x, z)

    def along(axis, by):
        at = dict(pos)
        at[axis] = pos[axis] + by
        return device(at["y"], core, at["x"], at["z"])

    greet([device(y, core, x + dx, z + dz) for dx, dz in OFFSETS] + [partner] + [along("y", b) for b in (1, 2, 3)])

    hop_id, slot = {}, {}
    for i, (_, _, hops) in enumerate(ROUTES):
        for k in range(len(hops)):
            hop_id[i, k] = len(hop_id)
            if k < len(hops) - 1:
                slot[i, k] = len(slot)
    copies = {}

    def launch(i, k, src):
        _, half, hops = ROUTES[i]
        gone_x, gone_z = (sum(h[a] for h in hops[:k]) for a in (0, 1))
        if k == len(hops) - 1:
            origin = lax.rem(x - gone_x + 4, 4) * 4 + lax.rem(z - gone_z + 4, 4)
            dst = arrived.at[pl.ds(origin * CAP + half * PIECE, PIECE)]
        else:
            dst = relay.at[pl.ds(slot[i, k] * PIECE, PIECE)]
        j = hop_id[i, k]
        copies[i, k] = pltpu.make_async_remote_copy(
            src, dst, send.at[j], recv.at[j],
            device_id=device(y, core, x + hops[k][0], z + hops[k][1]), device_id_type=MESH,
        )
        copies[i, k].start()

    before, after = lax.rem(me + 15, 16), lax.rem(me + 1, 16)
    left = device(y, core, before // 4, lax.rem(before, 4))
    right = device(y, core, after // 4, lax.rem(after, 4))
    first = pltpu.make_async_remote_copy(
        cot.at[pl.ds(0, 16)], edge.at[0], edge_sem.at[0], edge_sem.at[1], device_id=left, device_id_type=MESH)
    last = pltpu.make_async_remote_copy(
        cot.at[pl.ds(FR - 16, 16)], edge.at[1], edge_sem.at[2], edge_sem.at[3], device_id=right, device_id_type=MESH)
    first.start()
    last.start()
    for i, ((dx, dz), half, _) in enumerate(ROUTES):
        to = lax.rem(x + dx, 4) * 4 + lax.rem(z + dz, 4)
        launch(i, 0, loader.at[pl.ds(to * CAP + half * PIECE, PIECE)])
    own = pltpu.make_async_copy(loader.at[pl.ds(me * CAP, CAP)], arrived.at[pl.ds(me * CAP, CAP)], local.at[0])
    get_cot = pltpu.make_async_copy(cot, cotv, local.at[1])
    get_wp = pltpu.make_async_copy(w_project, wp, local.at[2])
    get_we = pltpu.make_async_copy(w_expand, we, local.at[3])
    get_small = [
        pltpu.make_async_copy(src, dst, local.at[6 + i])
        for i, (src, dst) in enumerate(((norm_gain_in, norm_gain), (taps_in, taps), (conv_gain_in, conv_gain)))
    ]
    for c in [get_cot, get_wp, own, get_we] + get_small:
        c.start()
    get_cot.wait()
    get_wp.wait()

    @pl.loop(0, 4)
    def _(k):
        r0 = pl.multiple_of(k * 256, 256)
        frame = r0 + lax.broadcasted_iota(jnp.int32, (256, 1), 0)
        tile = cotv[pl.ds(r0, 256)]
        tile = jnp.where(frame < live, tile, jnp.zeros_like(tile))
        cotv[pl.ds(r0, 256)] = tile
        gsw[pl.ds(pl.multiple_of(r0 + 16, 16), 256)] = contract_cols(tile, wp[...])

    gainsum[...] = jnp.zeros_like(gainsum)
    total[...] = jnp.zeros_like(total)
    small[...] = jnp.zeros_like(small)

    column = [counts[j, me] for j in range(16)]
    lane = lax.broadcasted_iota(jnp.int32, (1, CAP), 1)

    def collect(offsets, fresh):
        origins, places = [], []
        for dx, dz in offsets:
            origin = lax.rem(x - dx + 4, 4) * 4 + lax.rem(z - dz + 4, 4)
            begin = count = jnp.int32(0)
            for j in range(16):
                begin = begin + jnp.where(j < origin, column[j], 0)
                count = count + jnp.where(j == origin, column[j], 0)
            origins.append(origin)
            places.append(jnp.where(lane < count, begin + lane, -1))
        places = jnp.concatenate(places, axis=1)

        @pl.loop(0, 4)
        def _(k):
            r0 = pl.multiple_of(k * 256, 256)
            frame = r0 + lax.broadcasted_iota(jnp.int32, (256, 1), 0)
            pick = jnp.where(frame == places, 1.0, 0.0).astype(BF16)
            rows = jnp.concatenate([arrived[pl.ds(pl.multiple_of(o * CAP, CAP), CAP)] for o in origins], axis=0)
            got = jnp.dot(pick, rows, preferred_element_type=F32)
            seq[pl.ds(r0, 256)] = got if fresh else seq[pl.ds(r0, 256)] + got

    def forward(k):
        for i, (_, _, hops) in enumerate(ROUTES):
            if k < len(hops):
                copies[i, k - 1].wait_recv()
                launch(i, k, relay.at[pl.ds(slot[i, k - 1] * PIECE, PIECE)])

    def arrive(steps, more, fresh):
        here = list(more)
        for i, (offset, _, hops) in enumerate(ROUTES):
            if len(hops) == steps:
                copies[i, steps - 1].wait_recv()
                if offset not in here:
                    here.append(offset)
        collect(here, fresh)

    forward(1)
    first.wait()
    last.wait()
    rim = jnp.concatenate([edge[0].astype(F32)[:HALO], edge[1].astype(F32)[16 - HALO :]], axis=0)
    frame = row_frames(FR, 2 * HALO)
    rim = jnp.where((frame < live) & (frame + me * FR >= 0), rim, 0.0).astype(BF16)
    rim = contract_cols(rim, wp[...])
    gsw[FR + 16 : FR + 24] = rim[:HALO]
    gsw[8:16] = rim[HALO:]
    own.wait()
    arrive(1, [(0, 0)], True)
    forward(2)
    arrive(2, [], False)
    forward(3)
    arrive(3, [], False)
    arrive(4, [], False)

    first = pltpu.make_async_remote_copy(
        seq.at[pl.ds(0, HALO)], seq.at[pl.ds(FR, HALO)], edge_sem.at[4], edge_sem.at[5], device_id=left, device_id_type=MESH)
    last = pltpu.make_async_remote_copy(
        seq.at[pl.ds(FR - HALO, HALO)], seq.at[pl.ds(FR + HALO, HALO)], edge_sem.at[6], edge_sem.at[7], device_id=right, device_id_type=MESH)
    first.start()
    last.start()
    for c in [get_we] + get_small:
        c.wait()

    @pl.loop(0, EXT // T1)
    def _(k):
        @pl.when(k == EXT // T1 - 1)
        def _():
            first.wait()
            last.wait()

        r0 = pl.multiple_of(k * T1, 16)
        at = pl.ds(r0, T1)
        center, inverse = moments(lambda n: seq[at, lanes(n)])
        mean_in[at], inverse_in[at] = center, inverse
        for n in range(D // CC):
            scaled[at, lanes(n)] = ((seq[at, lanes(n)] - center) * inverse * norm_gain[:, lanes(n)]).astype(BF16)
        frame = row_frames(r0, T1)
        valid = (frame < live) & (frame + me * FR >= 0)

        @pl.loop(0, 2)
        def _(h):
            c = pl.multiple_of(h * 512, 512)
            s = scaled[pl.ds(r0, T1)]
            a = jnp.dot(s, we[:, pl.ds(c, 512)], preferred_element_type=F32)
            b = jax.nn.sigmoid(jnp.dot(s, we[:, pl.ds(D + c, 512)], preferred_element_type=F32))
            lin[pl.ds(r0, T1), pl.ds(c, 512)] = a
            gate[pl.ds(r0, T1), pl.ds(c, 512)] = b
            glu[pl.ds(pl.multiple_of(r0 + 16, 16), T1), pl.ds(c, 512)] = jnp.where(valid, a * b, 0.0).astype(BF16).astype(F32)

    glu[pl.ds(8, 8)] = glu[pl.ds(16 + FR + HALO, 8)]
    glu[pl.ds(0, 8)] = jnp.zeros((8, D), F32)

    @pl.loop(0, D // CC)
    def _(n):
        c = pl.ds(pl.multiple_of(n * CC, CC), CC)
        tap = [jnp.broadcast_to(taps[t : t + 1, c], (8, CC)) for t in range(KER)]

        @pl.loop(0, EXT // RC)
        def _(k):
            r0 = pl.multiple_of(k * RC, 16)
            wide = glu[pl.ds(r0, RC + 16), c]
            acc = None
            for t in range(KER):
                term = (wide[4 + t : 4 + t + RC].reshape(RC // 8, 8, CC) * tap[t]).reshape(RC, CC)
                acc = term if acc is None else acc + term
            at = pl.ds(pl.multiple_of(r0 + 8, 8), RC)
            dgrad[at, c] = acc
            total[at] += acc

    def middle(at, rows):
        center = spread(total[at])
        square = None
        for n in range(D // CC):
            off = dgrad[at, lanes(n)] - center
            square = off * off if square is None else square + off * off
        inverse = lax.rsqrt(spread(square) + EPS)
        sum_h = sum_hn = None
        for n in range(D // CC):
            gain = conv_gain[:, lanes(n)]
            normed = (dgrad[at, lanes(n)] - center) * inverse
            sc = normed * gain
            sig = jax.nn.sigmoid(sc)
            sw = sc * sig
            gsc = gsw[at, lanes(n)] * (sig + sw * (1.0 - sig))
            h = gsc * gain
            hn = h * normed
            gsw[at, lanes(n)] = h
            dgrad[at, lanes(n)] = normed
            sum_h = h if sum_h is None else sum_h + h
            sum_hn = hn if sum_hn is None else sum_hn + hn
            if rows is not None:
                swished[rows, lanes(n)] = sw.astype(BF16)
                gainsum[0, :, lanes(n)] += fold(gsc * normed)
        sum_h, sum_hn = spread(sum_h), spread(sum_hn)
        for n in range(D // CC):
            dgrad[at, lanes(n)] = inverse * (gsw[at, lanes(n)] - sum_h - dgrad[at, lanes(n)] * sum_hn)

    @pl.loop(0, FR // RM)
    def _(k):
        r0 = pl.multiple_of(k * RM, RM)
        middle(pl.ds(pl.multiple_of(r0 + 16, 16), RM), pl.ds(r0, RM))

    middle(slice(8, 16), None)
    middle(slice(FR + 16, FR + 24), None)

    def block(p, c, cols):
        c = lax.rem(c + 4, 4)
        index = (c, slice(None)) if ORDERS[p][0] == "x" else (slice(None), c)
        return index + (slice(None), slice(None), cols)

    def cell(p, c):
        c = lax.rem(c + 4, 4)
        return (x, c) if ORDERS[p][0] == "x" else (c, z)

    def low_high(p):
        return pl.ds(0, WIDTH[p] // 2), pl.ds(WIDTH[p] // 2, WIDTH[p] // 2)

    flying, crossing, climbing, pairs, finals, done = {}, {}, {}, {}, {}, []

    def pair_start(p):
        pairs[p] = pltpu.make_async_remote_copy(
            away[p], pair[p], pair_sem.at[0, p], pair_sem.at[1, p], device_id=partner, device_id_type=MESH)
        pairs[p].start()

    def pair_finish(p):
        pairs[p].wait_recv()

        @pl.loop(0, 16)
        def _(i):
            a, b = i // 4, lax.rem(i, 4)
            part[p][a, b] = (part[p][a, b].astype(F32) + pair[p][a, b].astype(F32)).astype(BF16)

    def step(p, n, at, dst, by):
        c = pltpu.make_async_remote_copy(
            part[p].at[at], dst, hop_sem.at[0, p, n], hop_sem.at[1, p, n],
            device_id=along(ORDERS[p][0], by), device_id_type=MESH)
        c.start()
        flying[p].append(c)
        done.append(c)

    def ring_start(p):
        m = pos[ORDERS[p][0]]
        lo, hi = low_high(p)
        flying[p] = []
        step(p, 0, block(p, m + 2, lo), hop1[p].at[0], 1)
        step(p, 1, block(p, m + 2, hi), hop1[p].at[1], -1)
        step(p, 2, block(p, m + 1, hi), hop2[p].at[0], 1)
        step(p, 3, block(p, m - 1, lo), hop2[p].at[1], -1)

    def ring_middle(p):
        m = pos[ORDERS[p][0]]
        for n, (by, cols) in enumerate(zip((1, -1), low_high(p))):
            flying[p][n].wait_recv()
            at = block(p, m + by, cols)
            part[p][at] = (part[p][at].astype(F32) + hop1[p][n].astype(F32)).astype(BF16)
            step(p, 4 + n, at, hop2[p].at[2 + n], by)

    def ring_end(p):
        m = pos[ORDERS[p][0]]
        for c in flying[p][2:]:
            c.wait_recv()
        low, high = (block(p, m, cols) for cols in low_high(p))
        part[p][low] = (part[p][low].astype(F32) + hop2[p][2].astype(F32) + hop2[p][1].astype(F32)).astype(BF16)
        part[p][high] = (part[p][high].astype(F32) + hop2[p][0].astype(F32) + hop2[p][3].astype(F32)).astype(BF16)
        crossing[p] = []
        for by in (2, 1, 3):
            c = pltpu.make_async_remote_copy(
                part[p].at[cell(p, pos[ORDERS[p][1]] + by)], cross[p].at[by - 1], cross_sem.at[0, p, by - 1], cross_sem.at[1, p, by - 1],
                device_id=along(ORDERS[p][1], by), device_id_type=MESH)
            c.start()
            crossing[p].append(c)
            done.append(c)

    def cross_end(p):
        for c in crossing[p]:
            c.wait_recv()
        total_here = part[p][cell(p, pos[ORDERS[p][1]])].astype(F32)
        for k in range(3):
            total_here = total_here + cross[p][k].astype(F32)
        tall[p][y] = total_here.astype(BF16)
        climbing[p] = []
        for by in (2, 1, 3):
            c = pltpu.make_async_remote_copy(
                tall[p].at[y], tall[p].at[y], tall_sem.at[0, p, by - 1], tall_sem.at[1, p, by - 1],
                device_id=along("y", by), device_id_type=MESH)
            c.start()
            climbing[p].append(c)
            done.append(c)

    def tall_end(p):
        for c in climbing[p]:
            c.wait_recv()
        t = [tall[p][k].astype(F32) for k in range(4)]
        mine = final.at[core, :, :, START[p] : START[p] + WIDTH[p]]
        mine[...] = (t[0] + t[1]) + (t[2] + t[3])
        finals[p] = pltpu.make_async_remote_copy(
            mine, mine, fin_sem.at[0, p], fin_sem.at[1, p], device_id=partner, device_id_type=MESH)
        finals[p].start()

    small_flying = {}

    def small_start(s, value):
        axis = "xzy"[s]
        buf = ring_small.at[s]
        buf[pos[axis]] = value
        small_flying[s] = []
        for by in (1, 2, 3):
            c = pltpu.make_async_remote_copy(
                buf.at[pos[axis]], buf.at[pos[axis]], sm_sem.at[0, 3 * s + by], sm_sem.at[1, 3 * s + by],
                device_id=along(axis, by), device_id_type=MESH)
            c.start()
            small_flying[s].append(c)

    def small_end(s):
        for c in small_flying[s]:
            c.wait()
        b = ring_small.at[s]
        return (b[0] + b[1]) + (b[2] + b[3])

    def project_grad(dst, half):
        @pl.loop(0, 4)
        def _(k):
            value = contract_rows(
                swished[:, pl.ds(pl.multiple_of(k * 256, 256), 256)], cotv[:, pl.ds(pl.multiple_of(half * 512, 512), 512)])
            dst[0][k] = value.astype(BF16).reshape(4, 4, 16, WIDTH[0])

    project_grad(away, 1 - core)
    pair_start(0)
    project_grad(part, core)

    def project(lo, hi):
        @pl.loop(lo, hi)
        def _(k):
            r0 = pl.multiple_of(k * 256, 256)
            frame = r0 + lax.broadcasted_iota(jnp.int32, (256, 1), 0)
            projected = jnp.dot(swished[pl.ds(r0, 256)], wp[...], preferred_element_type=F32)
            swished[pl.ds(r0, 256)] = jnp.where(frame < live, seq[pl.ds(r0, 256)] + projected, 0.0).astype(BF16)

    pair_finish(0)
    ring_start(0)

    def conv_back(lo, hi):
        @pl.loop(lo, hi)
        def _(n):
            c = pl.ds(pl.multiple_of(n * CC, CC), CC)
            tap = [jnp.broadcast_to(taps[t : t + 1, c], (8, CC)) for t in range(KER)]

            def rows(k, sums):
                r0 = pl.multiple_of(k * RB, RB)
                frame = r0 + lax.broadcasted_iota(jnp.int32, (RB, 1), 0)
                wide = dgrad[pl.ds(pl.multiple_of(r0 + 8, 8), RB + 16), c]
                mid = glu[pl.ds(pl.multiple_of(r0 + 16, 16), RB), c]
                acc, new = None, []
                for t in range(KER):
                    shifted = wide[12 - t : 12 - t + RB]
                    term = (shifted.reshape(RB // 8, 8, CC) * tap[t]).reshape(RB, CC)
                    acc = term if acc is None else acc + term
                    new.append(sums[t] + fold(mid * shifted))
                a = lin[pl.ds(r0, RB), c]
                b = gate[pl.ds(r0, RB), c]
                gg = jnp.where(frame < live, acc, 0.0) * b
                arrived[pl.ds(r0, RB), c] = gg.astype(BF16)
                arrived[pl.ds(pl.multiple_of(FR + r0, RB), RB), c] = (gg * a * (1.0 - b)).astype(BF16)
                return tuple(new)

            sums = lax.fori_loop(0, FR // RB, rows, tuple(jnp.zeros((8, CC), F32) for _ in range(KER)))
            for t in range(KER):
                small[t : t + 1, c] = jnp.sum(sums[t], axis=0, keepdims=True)

    def expand_grad(dst, p, half):
        first_col = START[p] - START[1]

        @pl.loop(0, 4)
        def _(k):
            value = contract_rows(
                scaled[pl.ds(0, FR), pl.ds(pl.multiple_of(k * 256, 256), 256)],
                arrived[pl.ds(pl.multiple_of(half * FR, FR), FR), first_col : first_col + WIDTH[p]])
            dst[p][k] = value.astype(BF16).reshape(4, 4, 16, WIDTH[p])

    conv_back(0, 3)
    ring_middle(0)
    conv_back(3, 6)
    expand_grad(away, 1, 1 - core)
    pair_start(1)
    ring_end(0)
    expand_grad(part, 1, core)
    conv_back(6, 8)
    pair_finish(1)
    ring_start(1)
    expand_grad(away, 2, 1 - core)
    pair_start(2)
    cross_end(0)
    expand_grad(part, 2, core)
    pair_finish(2)
    ring_start(2)
    tall_end(0)

    def input_grad(lo, hi):
        @pl.loop(lo, hi)
        def _(k):
            r0 = pl.multiple_of(k * 256, 256)
            grad_scaled = contract_cols(arrived[pl.ds(r0, 256)], we[:, :D]) + contract_cols(
                arrived[pl.ds(pl.multiple_of(FR + r0, 256), 256)], we[:, D:])
            at = pl.ds(r0, 256)
            gsw[at] = grad_scaled
            center, inverse = mean_in[at], inverse_in[at]
            sum_g = sum_gn = None
            for n in range(D // CC):
                normed = (seq[at, lanes(n)] - center) * inverse
                product = gsw[at, lanes(n)] * normed
                gainsum[1, :, lanes(n)] += fold(product)
                g = gsw[at, lanes(n)] * norm_gain[:, lanes(n)]
                gn = product * norm_gain[:, lanes(n)]
                sum_g = g if sum_g is None else sum_g + g
                sum_gn = gn if sum_gn is None else sum_gn + gn
            sum_g, sum_gn = spread(sum_g), spread(sum_gn)
            for n in range(D // CC):
                normed = (seq[at, lanes(n)] - center) * inverse
                g = gsw[at, lanes(n)] * norm_gain[:, lanes(n)]
                cotv[at, lanes(n)] = (
                    cotv[at, lanes(n)].astype(F32) + inverse * (g - sum_g - normed * sum_gn)).astype(BF16)

    input_grad(0, 2)
    ring_middle(1)
    ring_middle(2)
    input_grad(2, 4)
    put_grad = pltpu.make_async_copy(cotv, grad_in, local.at[5])
    put_grad.start()
    small[9:10] = jnp.sum(gainsum[1], axis=0, keepdims=True)
    small[10:11] = jnp.sum(gainsum[0], axis=0, keepdims=True)
    there = pl.multiple_of((1 - core) * 512, 512)
    here = pl.multiple_of(core * 512, 512)
    small_pair = pltpu.make_async_remote_copy(
        small.at[:, pl.ds(there, 512)], pair_small, sm_sem.at[0, 0], sm_sem.at[1, 0], device_id=partner, device_id_type=MESH)
    small_pair.start()
    ring_end(2)
    small_pair.wait()
    small_start(0, small[:, pl.ds(here, 512)] + pair_small[...])
    ring_end(1)
    project(0, 2)
    cross_end(2)
    small_start(1, small_end(0))
    project(2, 4)
    put_out = pltpu.make_async_copy(swished, layer_out, local.at[4])
    put_out.start()
    cross_end(1)
    small_start(2, small_end(1))
    tall_end(2)
    tall_end(1)
    full_small[core] = small_end(2)
    small_last = pltpu.make_async_remote_copy(
        full_small.at[core], full_small.at[core], sm_sem.at[0, 10], sm_sem.at[1, 10], device_id=partner, device_id_type=MESH)
    small_last.start()
    for c in list(copies.values()) + list(pairs.values()) + done:
        c.wait_send()
    put_out.wait()
    put_grad.wait()
    small_last.wait()
    out_small[:, 0:512] = full_small[0]
    out_small[:, 512:1024] = full_small[1]
    for c in finals.values():
        c.wait()
    out_sum[...] = final[...]


def finish_kernel(layer_in, grad_src, sums, small, layer_out, grad_in, expand, project, taps, norm_gain, conv_gain):
    layer_out[0] = layer_in[...]
    grad_in[0] = grad_src[...]

    @pl.when(pl.program_id(0) == 0)
    def _():
        for k in range(4):
            for c in range(2):
                rows = sums[c, k]
                project[k * 16 : k * 16 + 16, c * 512 : (c + 1) * 512] = rows[:, :512]
                expand[k * 16 : k * 16 + 16, c * 1024 : (c + 1) * 1024] = rows[:, 512:]
        taps[...] = small[0:KER]
        norm_gain[...] = small[9:10]
        conv_gain[...] = small[10:11]


def per_device(
    loader_rows, frame_counts, lengths, cotangent, norm_gain, w_expand, conv_taps, conv_gain, w_project,
):
    any_space = pl.BlockSpec(memory_space=pl.ANY)
    vmem = pl.BlockSpec(memory_space=pltpu.VMEM)
    smem = pl.BlockSpec(memory_space=pltpu.SMEM)

    def each(shape_of):
        return tuple(pltpu.VMEM(shape_of(w), BF16) for w in WIDTH)

    layer_out, grad_in, _, sums, small = pl.pallas_call(
        kernel,
        out_shape=[
            jax.ShapeDtypeStruct((FR, D), BF16),
            jax.ShapeDtypeStruct((FR, D), BF16),
            jax.ShapeDtypeStruct((N_RELAY * PIECE, D), BF16),
            jax.ShapeDtypeStruct((2, 4, 16, sum(WIDTH)), F32),
            jax.ShapeDtypeStruct((16, D), F32),
        ],
        in_specs=[any_space, any_space, smem, smem] + [any_space] * 5,
        out_specs=[any_space] * 3 + [vmem] * 2,
        scratch_shapes=[
            pltpu.VMEM((16 * CAP, D), BF16),
            pltpu.VMEM((FR, D), BF16),
            pltpu.VMEM((2, 16, D), BF16),
            pltpu.VMEM((D, D), BF16),
            pltpu.VMEM((D, 2 * D), BF16),
            pltpu.VMEM((EXT, D), F32),
            pltpu.VMEM((FR + 32, D), F32),
            pltpu.VMEM((FR + 32, D), F32),
            pltpu.VMEM((FR + 32, D), F32),
            pltpu.VMEM((EXT, D), F32),
            pltpu.VMEM((EXT, D), F32),
            pltpu.VMEM((EXT, D), BF16),
            pltpu.VMEM((FR, D), BF16),
            pltpu.VMEM((2, 8, D), F32),
            pltpu.VMEM((16, D), F32),
            pltpu.VMEM((FR + 32, CC), F32),
            pltpu.VMEM((EXT, CC), F32),
            pltpu.VMEM((EXT, CC), F32),
            pltpu.VMEM((1, D), F32),
            pltpu.VMEM((KER, D), F32),
            pltpu.VMEM((1, D), F32),
            *[each(lambda w: (4, 4, 4, 16, w)) for _ in range(3)],
            each(lambda w: (2, 4, 4, 16, w // 2)),
            each(lambda w: (4, 4, 4, 16, w // 2)),
            each(lambda w: (3, 4, 16, w)),
            each(lambda w: (4, 4, 16, w)),
            pltpu.VMEM((2, 4, 16, sum(WIDTH)), F32),
            pltpu.VMEM((16, 512), F32),
            pltpu.VMEM((3, 4, 16, 512), F32),
            pltpu.VMEM((2, 16, 512), F32),
            DMA((N_HOPS,)),
            DMA((N_HOPS,)),
            DMA((9,)),
            DMA((8,)),
            DMA((2, 3)),
            DMA((2, 3, 6)),
            DMA((2, 3, 3)),
            DMA((2, 3, 3)),
            DMA((2, 3)),
            DMA((2, 11)),
        ],
        compiler_params=pltpu.CompilerParams(collective_id=0, has_side_effects=True, vmem_limit_bytes=VMEM_LIMIT),
    )(
        loader_rows[0], cotangent[0], frame_counts[0], lengths, norm_gain[None], w_expand, conv_taps, conv_gain[None],
        w_project,
    )
    layer_out, grad_in, expand, project, taps, norm_gain, conv_gain = pl.pallas_call(
        finish_kernel,
        out_shape=[
            jax.ShapeDtypeStruct((1, FR, D), BF16),
            jax.ShapeDtypeStruct((1, FR, D), BF16),
            jax.ShapeDtypeStruct((D // 16, 2 * D), F32),
            jax.ShapeDtypeStruct((D // 16, D), F32),
            jax.ShapeDtypeStruct((KER, D), F32),
            jax.ShapeDtypeStruct((1, D), F32),
            jax.ShapeDtypeStruct((1, D), F32),
        ],
        grid=(2,),
        in_specs=[pl.BlockSpec((FR // 2, D), lambda i: (i, 0))] * 2 + [vmem] * 2,
        out_specs=[pl.BlockSpec((1, FR // 2, D), lambda i: (0, i, 0))] * 2 + [vmem] * 5,
    )(layer_out, grad_in, sums, small)
    return layer_out, grad_in, expand, project, taps, norm_gain[0], conv_gain[0]


def solution(mesh):
    return jax.shard_map(
        per_device,
        mesh=mesh,
        in_specs=(
            P("rec", "tm", None), P("rec", None, None), P("rec"), P("rec", "tm", None),
            P(), P(), P(), P(), P(),
        ),
        out_specs=(
            P("rec", "tm", None), P("rec", "tm", None), P("tm", None), P("tm", None), P(), P(), P(),
        ),
        check_vma=False,
    )
```
